128 devices in a mesh: seq: 4 (over z), mem: 32 (over x, y, core).
Axes of the slice: x: 4, y: 4, z: 4, core: 2. Of those that a mesh axis runs over, the one named last changes fastest.
Arguments:
- queries: bfloat16 [32, 512, 1024], P('mem', 'seq'), may hold values from -24 to 24
- keys: bfloat16 [32, 512, 1024], P('mem', 'seq'), may hold values from -8 to 8
- values: bfloat16 [32, 512, 1024], P('mem', 'seq'), may hold values from -6 to 6
- mem_keys: bfloat16 [65536, 1024], P(('seq', 'mem')), may hold values from -8 to 8
- mem_values: bfloat16 [65536, 1024], P(('seq', 'mem')), may hold values from -6 to 6
- knn_index: int32 [32, 512, 8, 32], P('mem', 'seq'), may hold values from 0 to 65535, as said below
- block_slot: int32 [1024], replicated, may hold values from 0 to 1023, as said below
- gate_bias: float32 [8], replicated, may hold values from -2 to 2
- w_out: bfloat16 [1024, 2048], replicated, may hold values from -0.1875 to 0.1875
Outputs:
- mixed: bfloat16 [32, 512, 2048], P('mem', 'seq')
The draws below stay inside these ranges and needn't reach their ends.
Inputs may be any that keep to these rules, and one draw needn't show every extreme that they name: `block_slot`: A permutation of the 1024 blocks. Storage row q lies on device q // 512 of seq+mem (seq slowest). `knn_index`: counting the lookups of one device (its tokens, all heads and ranks) by the device that stores the row, no device gets more than 384; some device gets exactly 384 from every device. Rows of one list may repeat.
All inputs are finite; a program needn't handle non-finite values.
Results may differ from the reference program's by a relative error of at most 0.011.
Values may be sent and summed in bfloat16 or wider, within the bound.
No kernel may reach another device: no remote copies, remote signals or barrier semaphores. Data moves between devices by JAX's collectives and lax.ppermute only.
A program may use at most 128 MiB of HBM per device.

```python
import jax
import jax.numpy as jnp
from jax import lax

D = 2048
HEADS = 8
HEAD = 128
TOPK = 32
TOK = 128
MEM_DEV = 512
SEQS = 32
SEQ_DEVS = 4
LEN = 512
DEV_COUNT = 128
HH = 1024
MEM = 65536
BLOCK = 64
NBLK = 1024
MEAN_LOAD = 256
CAP = 384


def shared_slots(key):
    return jax.random.permutation(jax.random.fold_in(key, 11), NBLK).astype(jnp.int32)


def draw_block_slot(key, part):
    slots = shared_slots(key)
    return slots


def draw_knn_index(key, part):
    slots = shared_slots(key)
    key = jax.random.fold_in(key, 5)
    inverse = jnp.zeros((NBLK,), jnp.int32).at[slots].set(jnp.arange(NBLK, dtype=jnp.int32))
    key_star, key_rank, key_shuffle, key_within = jax.random.split(key, 4)
    total = TOK * HEADS * TOPK
    star = jax.random.randint(key_star, (), 0, DEV_COUNT)
    ranks = jax.vmap(lambda k: jax.random.permutation(k, DEV_COUNT))(jax.random.split(key_rank, DEV_COUNT)).astype(jnp.int32)
    owner_ids = jnp.arange(DEV_COUNT, dtype=jnp.int32)[None, :]
    star_rank = ranks[:, star][:, None]
    ranks = jnp.where(owner_ids == star, 0, jnp.where(ranks < star_rank, ranks + 1, ranks))
    owner_by_rank = jnp.argsort(ranks, axis=1, stable=True).astype(jnp.int32)
    hot = DEV_COUNT // 2
    cold = MEAN_LOAD // 2
    spot = jnp.arange(total, dtype=jnp.int32)
    rank_of = jnp.where(spot < hot * CAP, spot // CAP, hot + (spot - hot * CAP) // cold)
    owners = jnp.take_along_axis(owner_by_rank, jnp.broadcast_to(rank_of[None, :], (DEV_COUNT, total)), axis=1)
    shuffles = jax.vmap(lambda k: jax.random.permutation(k, total))(jax.random.split(key_shuffle, DEV_COUNT)).astype(jnp.int32)
    owners = jnp.take_along_axis(owners, shuffles, axis=1)
    within = jax.random.randint(key_within, (DEV_COUNT, total), 0, MEM_DEV)
    storage = owners * MEM_DEV + within
    logical = jnp.take(inverse, storage // BLOCK) * BLOCK + storage % BLOCK
    logical = logical.reshape(SEQ_DEVS, SEQS, TOK, HEADS, TOPK).transpose(1, 0, 2, 3, 4)
    return logical.reshape(SEQS, LEN, HEADS, TOPK).astype(jnp.int32)


def draw_queries(key, part):
    key = jax.random.fold_in(key, 7)
    key_base = jax.random.fold_in(key, 0)
    base = jnp.clip(jax.random.normal(key_base, (SEQS, LEN, HEADS * HEAD), jnp.float32), -6.0, 6.0)
    return base.astype(jnp.bfloat16)


def draw_keys(key, part):
    key = jax.random.fold_in(key, 9)
    key_base = jax.random.fold_in(key, 0)
    base = jnp.clip(jax.random.normal(key_base, (SEQS, LEN, HEADS * HEAD), jnp.float32), -6.0, 6.0)
    return base.astype(jnp.bfloat16)


def draw_mem_keys(key, part):
    key = jax.random.fold_in(key, 13)
    key_base = jax.random.fold_in(key, 0)
    base = jnp.clip(jax.random.normal(key_base, (MEM, HEADS * HEAD), jnp.float32), -6.0, 6.0)
    return base.astype(jnp.bfloat16)


def level_of(key, shape, cuts, least, top_value):
    gain, own = 1.0, jax.random.fold_in(key, 6)
    for dim, shards_of in cuts:
        heights = jnp.exp(jax.random.uniform(jax.random.fold_in(own, dim), (shards_of,), jnp.float32, least / len(cuts), top_value / len(cuts)))
        gain = gain * jnp.repeat(heights, shape[dim] // shards_of).reshape([-1 if axis == dim else 1 for axis in range(len(shape))])
    return gain


def bell_draw(key, shape, width, bound, shards=(), kind=jnp.bfloat16):
    values = jax.random.normal(key, shape, jnp.float32) * width
    if len(shards) > 0:
        values = level_of(key, shape, shards, -0.22, 0.18) * values
    return jnp.clip(values, min=-bound, max=bound).astype(kind)


def setup_inputs(seed: int = 0) -> dict:
    key_list = jax.random.split(jax.random.key(seed), 10)
    return {
        "queries": draw_queries(jax.random.fold_in(key_list[9], 71), 0),
        "keys": draw_keys(jax.random.fold_in(key_list[9], 71), 0),
        "values": bell_draw(key_list[2], (SEQS, LEN, HH), 1.0, 6.0, ((0, 32), (1, 4))),
        "mem_keys": draw_mem_keys(jax.random.fold_in(key_list[9], 71), 0),
        "mem_values": bell_draw(key_list[4], (MEM, HH), 1.0, 6.0, ((0, 128),)),
        "knn_index": draw_knn_index(jax.random.fold_in(key_list[9], 71), 0),
        "block_slot": draw_block_slot(jax.random.fold_in(key_list[9], 71), 0),
        "gate_bias": jnp.clip(jax.random.uniform(key_list[7], (HEADS,), jnp.float32, -2.0, 2.0), -2.0, 2.0),
        "w_out": bell_draw(key_list[8], (HH, D), HH ** -0.5, 0.1875),
    }


def one_segment(table, block_slot, gate, w_out, parts):
    queries, keys, values, knn_index = parts
    scale = HEAD ** -0.5
    q = queries.reshape(LEN, HEADS, HEAD).astype(jnp.float32)
    k = keys.reshape(LEN, HEADS, HEAD).astype(jnp.float32)
    v = values.reshape(LEN, HEADS, HEAD).astype(jnp.float32)
    scores = jnp.einsum("qhd,khd->hqk", q, k) * scale
    position = jnp.arange(LEN)
    scores = jnp.where(position[None, None, :] <= position[None, :, None], scores, -jnp.inf)
    probs = jax.nn.softmax(scores, axis=-1).astype(jnp.bfloat16)
    local_out = jnp.einsum("hqk,khd->qhd", probs.astype(jnp.float32), v)
    storage = jnp.take(block_slot, knn_index // BLOCK) * BLOCK + knn_index % BLOCK
    code = storage * HEADS + jnp.arange(HEADS, dtype=jnp.int32)[None, :, None]
    fetched = jnp.take(table, code, axis=0).astype(jnp.float32)
    mem_k = fetched[..., :HEAD]
    mem_v = fetched[..., HEAD:]
    mem_scores = jnp.einsum("thd,thkd->thk", q, mem_k) * scale
    mem_probs = jax.nn.softmax(mem_scores, axis=-1).astype(jnp.bfloat16)
    mem_out = jnp.einsum("thk,thkd->thd", mem_probs.astype(jnp.float32), mem_v)
    combined = (gate * mem_out + (1.0 - gate) * local_out).astype(jnp.bfloat16)
    return jnp.dot(combined.reshape(LEN, HEADS * HEAD), w_out, preferred_element_type=jnp.float32).astype(jnp.bfloat16)


def reference(queries, keys, values, mem_keys, mem_values, knn_index, block_slot, gate_bias, w_out):
    table = jnp.concatenate([mem_keys.reshape(MEM * HEADS, HEAD), mem_values.reshape(MEM * HEADS, HEAD)], axis=1)
    gate = jax.nn.sigmoid(gate_bias.astype(jnp.float32))[None, :, None]
    return lax.map(lambda parts: one_segment(table, block_slot, gate, w_out, parts), (queries, keys, values, knn_index))
```

```python
import functools

import jax
import jax.numpy as jnp
from jax import lax
from jax.experimental import pallas as pl
from jax.experimental.pallas import tpu as pltpu
from jax.sharding import PartitionSpec as P

DEVS = 128
TOK = 128
HEADS = 8
HEAD = 128
TOPK = 32
MEM_DEV = 512
BLOCK = 64
CAP = 384
PART = 128
PARTS = CAP // PART
GROUP = 8
BATCH = 8
ROWS = 256
NT = (((1,), (1,)), ((), ()))


def one_hot(mask):
    return jnp.where(mask, 1.0, 0.0).astype(jnp.bfloat16)


def route_kernel(look_ref, slot_ref, req_ref, store, total, slots, parts):
    table = [jnp.broadcast_to(slot_ref[r : r + 1, :], (8, 128)) for r in range(8)]

    def translate(i, carry):
        base = pl.multiple_of(i * 8, 8)
        for half in range(ROWS // 128):
            look = look_ref[pl.ds(base, 8), half * 128 : (half + 1) * 128]
            blk = look >> 6
            low = blk & 127
            high = blk >> 7
            place = jnp.zeros((8, 128), jnp.int32)
            for r in range(8):
                place = jnp.where(high == r, jnp.take_along_axis(table[r], low, axis=1), place)
            store[pl.ds(base, 8), half * 128 : (half + 1) * 128] = place * BLOCK + (look & (BLOCK - 1))
        return carry

    lax.fori_loop(0, look_ref.shape[0] // 8, translate, 0)
    total[...] = jnp.zeros_like(total)
    upper = one_hot(
        lax.broadcasted_iota(jnp.int32, (ROWS, ROWS), 0) <= lax.broadcasted_iota(jnp.int32, (ROWS, ROWS), 1)
    )
    owners = lax.broadcasted_iota(jnp.int32, (DEVS, ROWS), 0)
    ranks = lax.broadcasted_iota(jnp.int32, (CAP, ROWS), 0)
    lane = lax.broadcasted_iota(jnp.int32, (1, ROWS), 1)
    batch = BATCH
    per_head = TOK * TOPK // ROWS

    def place(i, run):
        base = pl.multiple_of(i * batch, batch)
        rows = store[pl.ds(base, batch), :]
        for b in range(batch):
            row = base + b
            head = row // per_head
            tok = (row % per_head) * (ROWS // TOPK) + lane // TOPK
            here = rows[b : b + 1, :]
            mine = jnp.where(owners == here // MEM_DEV, 1.0, 0.0)
            count = jnp.dot(mine.astype(jnp.bfloat16), upper, preferred_element_type=jnp.float32) + run
            rank = jnp.sum(mine * count, axis=0, keepdims=True).astype(jnp.int32) - 1
            run = jnp.broadcast_to(count[:, ROWS - 1 :], (DEVS, ROWS))
            span = slice(b * ROWS, (b + 1) * ROWS)
            slots[:, span] = one_hot(ranks == rank)
            local = here & (MEM_DEV - 1)
            first = (local & 255).astype(jnp.float32)
            second = ((local >> 8) + 2 * tok).astype(jnp.float32)
            parts[0:DEVS, span] = (mine * first).astype(jnp.bfloat16)
            parts[DEVS : 2 * DEVS, span] = (mine * second).astype(jnp.bfloat16)
            parts[2 * DEVS :, span] = (mine * (head + 1).astype(jnp.float32)).astype(jnp.bfloat16)
        total[...] += lax.dot_general(parts[...], slots[...], NT, preferred_element_type=jnp.float32)
        return run

    lax.fori_loop(0, look_ref.shape[0] // batch, place, jnp.zeros((DEVS, ROWS), jnp.float32))
    first = total[0:DEVS, :].astype(jnp.int32)
    second = total[DEVS : 2 * DEVS, :].astype(jnp.int32)
    third = total[2 * DEVS :, :].astype(jnp.int32)
    local = first + (second & 1) * 256
    query = (third - 1) * TOK + (second >> 1)
    req_ref[...] = jnp.where(third > 0, query * MEM_DEV + local, -1)


def route(lookups, block_slot):
    return pl.pallas_call(
        route_kernel,
        out_shape=jax.ShapeDtypeStruct((DEVS, CAP), jnp.int32),
        scratch_shapes=[
            pltpu.VMEM((TOK * HEADS * TOPK // ROWS, ROWS), jnp.int32),
            pltpu.VMEM((3 * DEVS, CAP), jnp.float32),
            pltpu.VMEM((CAP, BATCH * ROWS), jnp.bfloat16),
            pltpu.VMEM((3 * DEVS, BATCH * ROWS), jnp.bfloat16),
        ],
        compiler_params=pltpu.CompilerParams(vmem_limit_bytes=32 * 1024 * 1024),
        name="route",
    )(lookups, block_slot.reshape(8, 128))


def pick_kernel(code_ref, mem_ref, out_ref, hot, head_of):
    code = jnp.transpose(code_ref[...])
    row_ids = lax.broadcasted_iota(jnp.int32, (PART, MEM_DEV), 1)
    for i in range(GROUP):
        col = code[:, i : i + 1]
        span = slice(i * PART, (i + 1) * PART)
        hot[span, :] = one_hot((col & (MEM_DEV - 1)) == row_ids)
        head_of[span, :] = jnp.broadcast_to(col >> 16, (PART, HEAD))
    for i in range(GROUP // 2):
        span = slice(i * 2 * PART, (i + 1) * 2 * PART)
        out = jnp.zeros((2 * PART, HEAD), jnp.float32)
        which = head_of[span, :]
        for pair in range(HEADS // 2):
            both = jnp.dot(
                hot[span, :], mem_ref[:, pair * 256 : (pair + 1) * 256], preferred_element_type=jnp.float32
            )
            out = jnp.where(which == 2 * pair, both[:, :HEAD], out)
            out = jnp.where(which == 2 * pair + 1, both[:, HEAD:], out)
        out_ref[2 * i : 2 * i + 2] = out.astype(jnp.bfloat16).reshape(2, PART, HEAD)


def pick(codes, mem, part):
    return pl.pallas_call(
        pick_kernel,
        grid=(DEVS // GROUP,),
        in_specs=[
            pl.BlockSpec((GROUP, PART), lambda g: (g, part)),
            pl.BlockSpec((MEM_DEV, HEADS * HEAD), lambda g: (0, 0)),
        ],
        out_specs=pl.BlockSpec((GROUP, PART, HEAD), lambda g: (g, 0, 0)),
        out_shape=jax.ShapeDtypeStruct((DEVS, PART, HEAD), jnp.bfloat16),
        scratch_shapes=[
            pltpu.VMEM((GROUP * PART, MEM_DEV), jnp.bfloat16),
            pltpu.VMEM((GROUP * PART, HEAD), jnp.int32),
        ],
        compiler_params=pltpu.CompilerParams(vmem_limit_bytes=32 * 1024 * 1024),
        name="pick",
    )(codes, mem)


def score_kernel(code_ref, query_ref, *refs):
    keys, out_ref = refs[:PARTS], refs[PARTS]
    step = pl.program_id(0)

    @pl.when(step == 0)
    def _():
        out_ref[...] = jnp.zeros_like(out_ref)

    tok_ids = lax.broadcasted_iota(jnp.int32, (PART, TOK), 1)
    lane = lax.broadcasted_iota(jnp.int32, (PART, DEVS), 1)
    for part in range(PARTS):
        code = jnp.transpose(code_ref[:, part * PART : (part + 1) * PART])
        acc = out_ref[part * PART : (part + 1) * PART, :]
        for i in range(GROUP):
            col = code[:, i : i + 1]
            which = jnp.broadcast_to(col >> 16, (PART, HEAD))
            hot = one_hot(((col >> 9) & (TOK - 1)) == tok_ids)
            query = jnp.zeros((PART, HEAD), jnp.float32)
            for pair in range(HEADS // 2):
                both = jnp.dot(
                    hot,
                    query_ref[i * TOK : (i + 1) * TOK, pair * 256 : (pair + 1) * 256],
                    preferred_element_type=jnp.float32,
                )
                query = jnp.where(which == 2 * pair, both[:, :HEAD], query)
                query = jnp.where(which == 2 * pair + 1, both[:, HEAD:], query)
            score = jnp.sum(query * keys[part][i].astype(jnp.float32), axis=1, keepdims=True)
            acc = jnp.where(lane == step * GROUP + i, score * HEAD ** (-0.5), acc)
        out_ref[part * PART : (part + 1) * PART, :] = acc


def score(codes, queries, keys):
    return pl.pallas_call(
        score_kernel,
        grid=(DEVS // GROUP,),
        in_specs=[
            pl.BlockSpec((GROUP, CAP), lambda g: (g, 0)),
            pl.BlockSpec((GROUP * TOK, HEADS * HEAD), lambda g: (g, 0)),
        ]
        + [pl.BlockSpec((GROUP, PART, HEAD), lambda g: (g, 0, 0))] * PARTS,
        out_specs=pl.BlockSpec((CAP, DEVS), lambda g: (0, 0)),
        out_shape=jax.ShapeDtypeStruct((CAP, DEVS), jnp.float32),
        compiler_params=pltpu.CompilerParams(vmem_limit_bytes=48 * 1024 * 1024),
        name="score",
    )(codes, queries, *keys)


def weigh_kernel(code_ref, score_ref, out_ref, top):
    step = 128
    tiles = HEADS * TOK // step

    def best(h, carry):
        base = pl.multiple_of(h * step, step)
        ids = lax.broadcasted_iota(jnp.int32, (step, PART), 0) + h * step

        def look(g, acc):
            rows = pl.ds(pl.multiple_of(g * GROUP, GROUP), GROUP)
            for part in range(PARTS):
                span = slice(part * PART, (part + 1) * PART)
                query = code_ref[rows, span] >> 9
                score = score_ref[rows, span]
                for i in range(GROUP):
                    acc = jnp.maximum(acc, jnp.where(ids == query[i : i + 1], score[i : i + 1], -jnp.inf))
            return acc

        acc = lax.fori_loop(0, DEVS // GROUP, look, jnp.full((step, PART), -jnp.inf, jnp.float32))
        top[pl.ds(base, step), :] = jnp.broadcast_to(jnp.max(acc, axis=1, keepdims=True), (step, PART))
        return carry

    lax.fori_loop(0, tiles, best, 0)

    def shift(g, carry):
        rows = pl.ds(pl.multiple_of(g * GROUP, GROUP), GROUP)
        for part in range(PARTS):
            span = slice(part * PART, (part + 1) * PART)
            query = code_ref[rows, span] >> 9
            highs = []
            for i in range(GROUP):
                found = jnp.zeros((step, PART), jnp.float32)
                for h in range(tiles):
                    ids = lax.broadcasted_iota(jnp.int32, (step, PART), 0) + h * step
                    found = jnp.where(ids == query[i : i + 1], top[h * step : (h + 1) * step, :], found)
                highs.append(jnp.sum(found, axis=0, keepdims=True))
            high = jnp.concatenate(highs, axis=0)
            out_ref[rows, span] = jnp.where(query >= 0, jnp.exp(score_ref[rows, span] - high), 0.0)
        return carry

    lax.fori_loop(0, DEVS // GROUP, shift, 0)


def weigh(codes, scores):
    return pl.pallas_call(
        weigh_kernel,
        out_shape=jax.ShapeDtypeStruct((DEVS, CAP), jnp.float32),
        scratch_shapes=[pltpu.VMEM((HEADS * TOK, PART), jnp.float32)],
        compiler_params=pltpu.CompilerParams(vmem_limit_bytes=32 * 1024 * 1024),
        name="weigh",
    )(codes, scores)


def mix_kernel(code_ref, weight_ref, value_ref, out_ref, spread, rows):
    step = pl.program_id(0)

    @pl.when(step == 0)
    def _():
        out_ref[...] = jnp.zeros_like(out_ref)
        rows[:, HEAD:] = jnp.ones((GROUP * PART, HEAD), jnp.bfloat16)

    for i in range(GROUP):
        span = slice(i * PART, (i + 1) * PART)
        rows[span, :HEAD] = value_ref[i]
        query = code_ref[i : i + 1, :] >> 9
        weight = weight_ref[i : i + 1, :]
        for h in range(HEADS):
            ids = lax.broadcasted_iota(jnp.int32, (TOK, PART), 0) + h * TOK
            spread[h * TOK : (h + 1) * TOK, span] = jnp.where(ids == query, weight, 0.0).astype(jnp.bfloat16)
    for h in range(HEADS // 2):
        span = slice(h * 2 * TOK, (h + 1) * 2 * TOK)
        out_ref[span, :] += jnp.dot(spread[span, :], rows[...], preferred_element_type=jnp.float32)


def mix(codes, weights, values, part):
    return pl.pallas_call(
        mix_kernel,
        grid=(DEVS // GROUP,),
        in_specs=[
            pl.BlockSpec((GROUP, PART), lambda g: (g, part)),
            pl.BlockSpec((GROUP, PART), lambda g: (g, part)),
            pl.BlockSpec((GROUP, PART, HEAD), lambda g: (g, 0, 0)),
        ],
        out_specs=pl.BlockSpec((HEADS * TOK, 2 * HEAD), lambda g: (0, 0)),
        out_shape=jax.ShapeDtypeStruct((HEADS * TOK, 2 * HEAD), jnp.float32),
        scratch_shapes=[
            pltpu.VMEM((HEADS * TOK, GROUP * PART), jnp.bfloat16),
            pltpu.VMEM((GROUP * PART, 2 * HEAD), jnp.bfloat16),
        ],
        compiler_params=pltpu.CompilerParams(vmem_limit_bytes=32 * 1024 * 1024),
        name="mix",
    )(codes, weights, values)


def shards(queries, keys, values, mem_keys, mem_values, knn_index, block_slot, gate_bias, w_out):
    every = ("seq", "mem")
    send = functools.partial(lax.all_to_all, axis_name=every, split_axis=0, concat_axis=0, tiled=True)
    scale = HEAD ** (-0.5)
    all_queries = lax.all_gather(queries[0], every, axis=0, tiled=True)
    whole_keys = lax.all_gather(keys[0], "seq", axis=0, tiled=True)
    whole_values = lax.all_gather(values[0], "seq", axis=0, tiled=True)

    lookups = knn_index[0].transpose(1, 0, 2).reshape(TOK * HEADS * TOPK // ROWS, ROWS)
    asked = route(lookups, block_slot)
    codes = send(asked)
    fetched = [send(pick(codes, mem_values, part)) for part in range(PARTS)]
    kept = [pick(codes, mem_keys, part) for part in range(PARTS)]
    scores = send(score(codes, all_queries, kept).T)
    weights = weigh(asked, scores)
    sums = sum(mix(asked, weights, fetched[part], part) for part in range(PARTS))
    mem_out = (sums[:, :HEAD] / sums[:, HEAD:]).reshape(HEADS, TOK, HEAD)

    query = queries[0].reshape(TOK, HEADS, HEAD)
    span = whole_keys.shape[0]
    key_rows = whole_keys.reshape(span, HEADS, HEAD)
    value_rows = whole_values.reshape(span, HEADS, HEAD)
    local = jnp.einsum("qhd,khd->hqk", query, key_rows, preferred_element_type=jnp.float32) * scale
    query_pos = lax.axis_index("seq") * TOK + jnp.arange(TOK, dtype=jnp.int32)
    key_pos = jnp.arange(span, dtype=jnp.int32)
    local = jnp.where(key_pos[None, None, :] <= query_pos[None, :, None], local, -jnp.inf)
    probs = jax.nn.softmax(local, axis=-1).astype(jnp.bfloat16)
    local_out = jnp.einsum("hqk,khd->hqd", probs, value_rows, preferred_element_type=jnp.float32)

    gate = jax.nn.sigmoid(gate_bias)[:, None, None]
    combined = (gate * mem_out + (1.0 - gate) * local_out).astype(jnp.bfloat16)
    combined = combined.transpose(1, 0, 2).reshape(TOK, HEADS * HEAD)
    mixed = jnp.dot(combined, w_out, preferred_element_type=jnp.float32).astype(jnp.bfloat16)
    return mixed[None]


def solution(mesh):
    return jax.shard_map(
        shards,
        mesh=mesh,
        in_specs=(
            P("mem", "seq", None),
            P("mem", "seq", None),
            P("mem", "seq", None),
            P(("seq", "mem"), None),
            P(("seq", "mem"), None),
            P("mem", "seq", None, None),
            P(),
            P(),
            P(),
        ),
        out_specs=P("mem", "seq", None),
        check_vma=False,
    )
```

```python
import functools

import jax
import jax.numpy as jnp
from jax import lax
from jax.experimental import pallas as pl
from jax.experimental.pallas import tpu as pltpu
from jax.sharding import PartitionSpec as P

DEVS = 128
TOK = 128
HEADS = 8
HEAD = 128
TOPK = 32
MEM_DEV = 512
BLOCK = 64
CAP = 384
PART = 128
PARTS = CAP // PART
GROUP = 8
BATCH = 8
ROWS = 256
WINDOW = 80
NT = (((1,), (1,)), ((), ()))


def one_hot(mask):
    return jnp.where(mask, 1.0, 0.0).astype(jnp.bfloat16)


def route_kernel(look_ref, slot_ref, req_ref, store, total, slots, parts, starts):
    table = [jnp.broadcast_to(slot_ref[r : r + 1, :], (8, 128)) for r in range(8)]

    def translate(i, carry):
        base = pl.multiple_of(i * 8, 8)
        for half in range(ROWS // 128):
            look = look_ref[pl.ds(base, 8), half * 128 : (half + 1) * 128]
            blk = look >> 6
            low = blk & 127
            high = blk >> 7
            place = jnp.zeros((8, 128), jnp.int32)
            for r in range(8):
                place = jnp.where(high == r, jnp.take_along_axis(table[r], low, axis=1), place)
            store[pl.ds(base, 8), half * 128 : (half + 1) * 128] = place * BLOCK + (look & (BLOCK - 1))
        return carry

    lax.fori_loop(0, look_ref.shape[0] // 8, translate, 0)
    total[...] = jnp.zeros_like(total)
    starts[...] = jnp.zeros_like(starts)
    heads = lax.broadcasted_iota(jnp.int32, starts.shape, 1)
    upper = one_hot(
        lax.broadcasted_iota(jnp.int32, (ROWS, ROWS), 0) <= lax.broadcasted_iota(jnp.int32, (ROWS, ROWS), 1)
    )
    owners = lax.broadcasted_iota(jnp.int32, (DEVS, ROWS), 0)
    ranks = lax.broadcasted_iota(jnp.int32, (CAP, ROWS), 0)
    lane = lax.broadcasted_iota(jnp.int32, (1, ROWS), 1)
    batch = BATCH
    per_head = TOK * TOPK // ROWS

    def place(i, run):
        base = pl.multiple_of(i * batch, batch)
        rows = store[pl.ds(base, batch), :]
        starts[...] = jnp.where((heads * per_head == base) & (heads < HEADS), run[:, :128], starts[...])
        for b in range(batch):
            row = base + b
            head = row // per_head
            tok = (row % per_head) * (ROWS // TOPK) + lane // TOPK
            here = rows[b : b + 1, :]
            mine = jnp.where(owners == here // MEM_DEV, 1.0, 0.0)
            count = jnp.dot(mine.astype(jnp.bfloat16), upper, preferred_element_type=jnp.float32) + run
            rank = jnp.sum(mine * count, axis=0, keepdims=True).astype(jnp.int32) - 1
            run = jnp.broadcast_to(count[:, ROWS - 1 :], (DEVS, ROWS))
            span = slice(b * ROWS, (b + 1) * ROWS)
            slots[:, span] = one_hot(ranks == rank)
            local = here & (MEM_DEV - 1)
            first = (local & 255).astype(jnp.float32)
            second = ((local >> 8) + 2 * tok).astype(jnp.float32)
            parts[0:DEVS, span] = (mine * first).astype(jnp.bfloat16)
            parts[DEVS : 2 * DEVS, span] = (mine * second).astype(jnp.bfloat16)
            parts[2 * DEVS :, span] = (mine * (head + 1).astype(jnp.float32)).astype(jnp.bfloat16)
        total[...] += lax.dot_general(parts[...], slots[...], NT, preferred_element_type=jnp.float32)
        return run

    run = lax.fori_loop(0, look_ref.shape[0] // batch, place, jnp.zeros((DEVS, ROWS), jnp.float32))
    first = total[0:DEVS, :].astype(jnp.int32)
    second = total[DEVS : 2 * DEVS, :].astype(jnp.int32)
    third = total[2 * DEVS :, :].astype(jnp.int32)
    local = first + (second & 1) * 256
    query = (third - 1) * TOK + (second >> 1)
    req_ref[:, :CAP] = jnp.where(third > 0, query * MEM_DEV + local, -1)
    req_ref[:, CAP:] = jnp.where(heads == HEADS, run[:, :128], starts[...]).astype(jnp.int32)


def route(lookups, block_slot):
    return pl.pallas_call(
        route_kernel,
        out_shape=jax.ShapeDtypeStruct((DEVS, CAP + 128), jnp.int32),
        scratch_shapes=[
            pltpu.VMEM((TOK * HEADS * TOPK // ROWS, ROWS), jnp.int32),
            pltpu.VMEM((3 * DEVS, CAP), jnp.float32),
            pltpu.VMEM((CAP, BATCH * ROWS), jnp.bfloat16),
            pltpu.VMEM((3 * DEVS, BATCH * ROWS), jnp.bfloat16),
            pltpu.VMEM((DEVS, 128), jnp.float32),
        ],
        compiler_params=pltpu.CompilerParams(vmem_limit_bytes=32 * 1024 * 1024),
        name="route",
    )(lookups, block_slot.reshape(8, 128))


def turn_kernel(query_ref, out_ref):
    for h in range(HEADS):
        span = slice(h * HEAD, (h + 1) * HEAD)
        out_ref[span, :] = jnp.transpose(query_ref[:, span].astype(jnp.float32)).astype(jnp.bfloat16)


def turn(queries):
    return pl.pallas_call(
        turn_kernel,
        out_shape=jax.ShapeDtypeStruct((HEADS * HEAD, TOK), jnp.bfloat16),
        name="turn",
    )(queries)


def pick_kernel(code_ref, start_ref, key_ref, value_ref, *refs):
    outs, kept_ref = refs[:PARTS], refs[PARTS]
    table, wanted, found, hot = refs[PARTS + 1 :]

    @pl.when(pl.program_id(0) == 0)
    def _():
        for h in range(HEADS):
            table[h, :, :HEAD] = key_ref[:, h * HEAD : (h + 1) * HEAD]
            table[h, :, HEAD:] = value_ref[:, h * HEAD : (h + 1) * HEAD]
        wanted[CAP:, :] = jnp.full((WINDOW, GROUP), -1, jnp.int32)

    for part in range(PARTS):
        span = slice(part * PART, (part + 1) * PART)
        code = jnp.transpose(code_ref[:, span])
        wanted[span, :] = (code & (MEM_DEV - 1)) + (code >> 16) * MEM_DEV
    found[...] = jnp.zeros_like(found)
    row_ids = lax.broadcasted_iota(jnp.int32, (WINDOW, MEM_DEV), 1)

    def one_head(h, carry):
        begins = [start_ref[i, h] // 8 * 8 for i in range(GROUP)]
        most = start_ref[0, h + 1] - begins[0]
        for i in range(1, GROUP):
            most = jnp.maximum(most, start_ref[i, h + 1] - begins[i])

        def one_window(w, carry):
            spans = []
            for i in range(GROUP):
                at = jnp.minimum(begins[i] + w * WINDOW, CAP)
                spans.append(pl.ds(pl.multiple_of(at, 8), WINDOW))
                col = wanted[spans[i], i : i + 1]
                hot[i * WINDOW : (i + 1) * WINDOW, :] = one_hot(col - h * MEM_DEV == row_ids)
            both = jnp.dot(hot[...], table[h], preferred_element_type=jnp.float32)
            for i in range(GROUP):
                found[i, spans[i], :] += both[i * WINDOW : (i + 1) * WINDOW, :]
            return carry

        return lax.fori_loop(0, (most + WINDOW - 1) // WINDOW, one_window, carry)

    lax.fori_loop(0, HEADS, one_head, 0)
    for i in range(GROUP):
        kept_ref[i] = found[i, :CAP, :HEAD].astype(jnp.bfloat16)
        for part in range(PARTS):
            outs[part][i] = found[i, part * PART : (part + 1) * PART, HEAD:].astype(jnp.bfloat16)


def pick(codes, mem_keys, mem_values):
    whole = pl.BlockSpec((MEM_DEV, HEADS * HEAD), lambda g: (0, 0))
    return pl.pallas_call(
        pick_kernel,
        grid=(DEVS // GROUP,),
        in_specs=[
            pl.BlockSpec((GROUP, CAP), lambda g: (g, 0)),
            pl.BlockSpec((GROUP, 128), lambda g: (g, CAP // 128), memory_space=pltpu.SMEM),
            whole,
            whole,
        ],
        out_specs=[pl.BlockSpec((GROUP, PART, HEAD), lambda g: (g, 0, 0))] * PARTS
        + [pl.BlockSpec((GROUP, CAP, HEAD), lambda g: (g, 0, 0))],
        out_shape=[jax.ShapeDtypeStruct((DEVS, PART, HEAD), jnp.bfloat16)] * PARTS
        + [jax.ShapeDtypeStruct((DEVS, CAP, HEAD), jnp.bfloat16)],
        scratch_shapes=[
            pltpu.VMEM((HEADS, MEM_DEV, 2 * HEAD), jnp.bfloat16),
            pltpu.VMEM((CAP + WINDOW, GROUP), jnp.int32),
            pltpu.VMEM((GROUP, CAP + WINDOW, 2 * HEAD), jnp.float32),
            pltpu.VMEM((GROUP * WINDOW, MEM_DEV), jnp.bfloat16),
        ],
        compiler_params=pltpu.CompilerParams(vmem_limit_bytes=40 * 1024 * 1024),
        name="pick",
    )(codes, codes, mem_keys, mem_values)


def score_kernel(code_ref, query_ref, key_ref, out_ref):
    tok_ids = lax.broadcasted_iota(jnp.int32, (TOK, CAP), 0)
    diagonal = lax.broadcasted_iota(jnp.int32, (PART, PART), 0) == lax.broadcasted_iota(
        jnp.int32, (PART, PART), 1
    )
    for i in range(GROUP):
        code = code_ref[i : i + 1, :]
        head = code >> 16
        hot = one_hot(((code >> 9) & (TOK - 1)) == tok_ids)
        each = jnp.dot(query_ref[i], hot, preferred_element_type=jnp.float32)
        query = jnp.zeros((HEAD, CAP), jnp.float32)
        for h in range(HEADS):
            query = jnp.where(head == h, each[h * HEAD : (h + 1) * HEAD, :], query)
        query = query.astype(jnp.bfloat16)
        for part in range(PARTS):
            span = slice(part * PART, (part + 1) * PART)
            cross = jnp.dot(key_ref[i, span, :], query[:, span], preferred_element_type=jnp.float32)
            score = jnp.sum(jnp.where(diagonal, cross, 0.0), axis=0, keepdims=True)
            out_ref[i : i + 1, span] = score * HEAD ** (-0.5)


def score(codes, queries, keys):
    return pl.pallas_call(
        score_kernel,
        grid=(DEVS // GROUP,),
        in_specs=[
            pl.BlockSpec((GROUP, CAP), lambda g: (g, 0)),
            pl.BlockSpec((GROUP, HEADS * HEAD, TOK), lambda g: (g, 0, 0)),
            pl.BlockSpec((GROUP, CAP, HEAD), lambda g: (g, 0, 0)),
        ],
        out_specs=pl.BlockSpec((GROUP, CAP), lambda g: (g, 0)),
        out_shape=jax.ShapeDtypeStruct((DEVS, CAP), jnp.float32),
        compiler_params=pltpu.CompilerParams(vmem_limit_bytes=40 * 1024 * 1024),
        name="score",
    )(codes, queries, keys)


def weigh_kernel(code_ref, score_ref, out_ref, top):
    step = 128
    tiles = HEADS * TOK // step

    def best(h, carry):
        base = pl.multiple_of(h * step, step)
        ids = lax.broadcasted_iota(jnp.int32, (step, PART), 0) + h * step

        def look(g, acc):
            rows = pl.ds(pl.multiple_of(g * GROUP, GROUP), GROUP)
            for part in range(PARTS):
                span = slice(part * PART, (part + 1) * PART)
                query = code_ref[rows, span] >> 9
                score = score_ref[rows, span]
                for i in range(GROUP):
                    acc = jnp.maximum(acc, jnp.where(ids == query[i : i + 1], score[i : i + 1], -jnp.inf))
            return acc

        acc = lax.fori_loop(0, DEVS // GROUP, look, jnp.full((step, PART), -jnp.inf, jnp.float32))
        top[pl.ds(base, step), :] = jnp.broadcast_to(jnp.max(acc, axis=1, keepdims=True), (step, PART))
        return carry

    lax.fori_loop(0, tiles, best, 0)

    def shift(g, carry):
        rows = pl.ds(pl.multiple_of(g * GROUP, GROUP), GROUP)
        for part in range(PARTS):
            span = slice(part * PART, (part + 1) * PART)
            query = code_ref[rows, span] >> 9
            highs = []
            for i in range(GROUP):
                found = jnp.zeros((step, PART), jnp.float32)
                for h in range(tiles):
                    ids = lax.broadcasted_iota(jnp.int32, (step, PART), 0) + h * step
                    found = jnp.where(ids == query[i : i + 1], top[h * step : (h + 1) * step, :], found)
                highs.append(jnp.sum(found, axis=0, keepdims=True))
            high = jnp.concatenate(highs, axis=0)
            out_ref[rows, span] = jnp.where(query >= 0, jnp.exp(score_ref[rows, span] - high), 0.0)
        return carry

    lax.fori_loop(0, DEVS // GROUP, shift, 0)


def weigh(codes, scores):
    return pl.pallas_call(
        weigh_kernel,
        out_shape=jax.ShapeDtypeStruct((DEVS, CAP), jnp.float32),
        scratch_shapes=[pltpu.VMEM((HEADS * TOK, PART), jnp.float32)],
        compiler_params=pltpu.CompilerParams(vmem_limit_bytes=32 * 1024 * 1024),
        name="weigh",
    )(codes, scores)


def mix_kernel(code_ref, weight_ref, value_ref, out_ref, spread, rows):
    step = pl.program_id(0)

    @pl.when(step == 0)
    def _():
        out_ref[...] = jnp.zeros_like(out_ref)
        rows[:, HEAD:] = jnp.ones((GROUP * PART, HEAD), jnp.bfloat16)

    for i in range(GROUP):
        span = slice(i * PART, (i + 1) * PART)
        rows[span, :HEAD] = value_ref[i]
        query = code_ref[i : i + 1, :] >> 9
        weight = weight_ref[i : i + 1, :]
        for h in range(HEADS):
            ids = lax.broadcasted_iota(jnp.int32, (TOK, PART), 0) + h * TOK
            spread[h * TOK : (h + 1) * TOK, span] = jnp.where(ids == query, weight, 0.0).astype(jnp.bfloat16)
    for h in range(HEADS // 2):
        span = slice(h * 2 * TOK, (h + 1) * 2 * TOK)
        out_ref[span, :] += jnp.dot(spread[span, :], rows[...], preferred_element_type=jnp.float32)


def mix(codes, weights, values, part):
    return pl.pallas_call(
        mix_kernel,
        grid=(DEVS // GROUP,),
        in_specs=[
            pl.BlockSpec((GROUP, PART), lambda g: (g, part)),
            pl.BlockSpec((GROUP, PART), lambda g: (g, part)),
            pl.BlockSpec((GROUP, PART, HEAD), lambda g: (g, 0, 0)),
        ],
        out_specs=pl.BlockSpec((HEADS * TOK, 2 * HEAD), lambda g: (0, 0)),
        out_shape=jax.ShapeDtypeStruct((HEADS * TOK, 2 * HEAD), jnp.float32),
        scratch_shapes=[
            pltpu.VMEM((HEADS * TOK, GROUP * PART), jnp.bfloat16),
            pltpu.VMEM((GROUP * PART, 2 * HEAD), jnp.bfloat16),
        ],
        compiler_params=pltpu.CompilerParams(vmem_limit_bytes=32 * 1024 * 1024),
        name="mix",
    )(codes, weights, values)


def shards(queries, keys, values, mem_keys, mem_values, knn_index, block_slot, gate_bias, w_out):
    every = ("seq", "mem")
    send = functools.partial(lax.all_to_all, axis_name=every, split_axis=0, concat_axis=0, tiled=True)
    scale = HEAD ** (-0.5)
    all_queries = lax.all_gather(turn(queries[0]), every, axis=0, tiled=True).reshape(DEVS, HEADS * HEAD, TOK)
    own = jnp.concatenate([keys[0], values[0]], axis=1)
    devices = lax.axis_size("seq")
    blocks = [own] + [
        lax.ppermute(own, "seq", [(i, i + back) for i in range(devices - back)]) for back in range(1, devices)
    ]

    lookups = knn_index[0].transpose(1, 0, 2).reshape(TOK * HEADS * TOPK // ROWS, ROWS)
    asked = route(lookups, block_slot)
    codes = send(asked)
    *picked, kept = pick(codes, mem_keys, mem_values)
    first = send(picked[0])
    first, kept = lax.optimization_barrier((first, kept))
    second = send(picked[1])
    scores = send(score(codes, all_queries, kept))
    scores, last = lax.optimization_barrier((scores, picked[2]))
    third = send(last)
    weights = weigh(asked, scores)
    sums = sum(mix(asked, weights, rows, part) for part, rows in enumerate((first, second, third)))
    mem_out = (sums[:, :HEAD] / sums[:, HEAD:]).reshape(HEADS, TOK, HEAD)

    query = queries[0].reshape(TOK, HEADS, HEAD)
    near = jnp.concatenate(blocks, axis=0)
    key_rows = near[:, : HEADS * HEAD].reshape(-1, HEADS, HEAD)
    value_rows = near[:, HEADS * HEAD :].reshape(-1, HEADS, HEAD)
    local = jnp.einsum("qhd,khd->hqk", query, key_rows, preferred_element_type=jnp.float32) * scale
    back = jnp.arange(near.shape[0], dtype=jnp.int32) // TOK
    within = jnp.arange(near.shape[0], dtype=jnp.int32) % TOK
    here = (back == 0)[None, :] & (within[None, :] <= jnp.arange(TOK, dtype=jnp.int32)[:, None])
    earlier = (back > 0) & (back <= lax.axis_index("seq"))
    local = jnp.where((here | earlier[None, :])[None], local, -jnp.inf)
    probs = jax.nn.softmax(local, axis=-1).astype(jnp.bfloat16)
    local_out = jnp.einsum("hqk,khd->hqd", probs, value_rows, preferred_element_type=jnp.float32)

    gate = jax.nn.sigmoid(gate_bias)[:, None, None]
    combined = (gate * mem_out + (1.0 - gate) * local_out).astype(jnp.bfloat16)
    combined = combined.transpose(1, 0, 2).reshape(TOK, HEADS * HEAD)
    mixed = jnp.dot(combined, w_out, preferred_element_type=jnp.float32).astype(jnp.bfloat16)
    return mixed[None]


def solution(mesh):
    return jax.shard_map(
        shards,
        mesh=mesh,
        in_specs=(
            P("mem", "seq", None),
            P("mem", "seq", None),
            P("mem", "seq", None),
            P(("seq", "mem"), None),
            P(("seq", "mem"), None),
            P("mem", "seq", None, None),
            P(),
            P(),
            P(),
        ),
        out_specs=P("mem", "seq", None),
        check_vma=False,
    )
```

```python
import functools

import jax
import jax.numpy as jnp
from jax import lax
from jax.experimental import pallas as pl
from jax.experimental.pallas import tpu as pltpu
from jax.sharding import PartitionSpec as P

DEVS = 128
TOK = 128
HEADS = 8
HEAD = 128
TOPK = 32
MEM_DEV = 512
BLOCK = 64
CAP = 384
PART = 128
PARTS = CAP // PART
GROUP = 8
BATCH = 8
ROWS = 256
WINDOW = 80
NT = (((1,), (1,)), ((), ()))


def one_hot(mask):
    return jnp.where(mask, 1.0, 0.0).astype(jnp.bfloat16)


def cost(micros):
    return pl.CostEstimate(flops=int(micros * 1e9), bytes_accessed=int(micros * 1e6), transcendentals=0)


def route_kernel(look_ref, slot_ref, req_ref, place_ref, store, total, slots, parts, starts):
    table = [jnp.broadcast_to(slot_ref[r : r + 1, :], (8, 128)) for r in range(8)]

    def translate(i, carry):
        base = pl.multiple_of(i * 8, 8)
        for half in range(ROWS // 128):
            look = look_ref[pl.ds(base, 8), half * 128 : (half + 1) * 128]
            blk = look >> 6
            low = blk & 127
            high = blk >> 7
            place = jnp.zeros((8, 128), jnp.int32)
            for r in range(8):
                place = jnp.where(high == r, jnp.take_along_axis(table[r], low, axis=1), place)
            store[pl.ds(base, 8), half * 128 : (half + 1) * 128] = place * BLOCK + (look & (BLOCK - 1))
        return carry

    lax.fori_loop(0, look_ref.shape[0] // 8, translate, 0)
    total[...] = jnp.zeros_like(total)
    starts[...] = jnp.zeros_like(starts)
    heads = lax.broadcasted_iota(jnp.int32, starts.shape, 1)
    upper = one_hot(
        lax.broadcasted_iota(jnp.int32, (ROWS, ROWS), 0) <= lax.broadcasted_iota(jnp.int32, (ROWS, ROWS), 1)
    )
    owners = lax.broadcasted_iota(jnp.int32, (DEVS, ROWS), 0)
    ranks = lax.broadcasted_iota(jnp.int32, (CAP, ROWS), 0)
    lane = lax.broadcasted_iota(jnp.int32, (1, ROWS), 1)
    batch = BATCH
    per_head = TOK * TOPK // ROWS

    def place(i, run):
        base = pl.multiple_of(i * batch, batch)
        rows = store[pl.ds(base, batch), :]
        starts[...] = jnp.where((heads * per_head == base) & (heads < HEADS), run[:, :128], starts[...])
        places = []
        for b in range(batch):
            row = base + b
            head = row // per_head
            tok = (row % per_head) * (ROWS // TOPK) + lane // TOPK
            here = rows[b : b + 1, :]
            owner = here // MEM_DEV
            mine = jnp.where(owners == owner, 1.0, 0.0)
            count = jnp.dot(mine.astype(jnp.bfloat16), upper, preferred_element_type=jnp.float32) + run
            rank = jnp.sum(mine * count, axis=0, keepdims=True).astype(jnp.int32) - 1
            run = jnp.broadcast_to(count[:, ROWS - 1 :], (DEVS, ROWS))
            places.append(owner * MEM_DEV + rank)
            span = slice(b * ROWS, (b + 1) * ROWS)
            slots[:, span] = one_hot(ranks == rank)
            local = here & (MEM_DEV - 1)
            first = (local & 255).astype(jnp.float32)
            second = ((local >> 8) + 2 * tok).astype(jnp.float32)
            parts[0:DEVS, span] = (mine * first).astype(jnp.bfloat16)
            parts[DEVS : 2 * DEVS, span] = (mine * second).astype(jnp.bfloat16)
            parts[2 * DEVS :, span] = (mine * (head + 1).astype(jnp.float32)).astype(jnp.bfloat16)
        total[...] += lax.dot_general(parts[...], slots[...], NT, preferred_element_type=jnp.float32)
        place_ref[pl.ds(base, batch), :] = jnp.concatenate(places, axis=0)
        return run

    run = lax.fori_loop(0, look_ref.shape[0] // batch, place, jnp.zeros((DEVS, ROWS), jnp.float32))
    first = total[0:DEVS, :].astype(jnp.int32)
    second = total[DEVS : 2 * DEVS, :].astype(jnp.int32)
    third = total[2 * DEVS :, :].astype(jnp.int32)
    local = first + (second & 1) * 256
    query = (third - 1) * TOK + (second >> 1)
    req_ref[:, :CAP] = jnp.where(third > 0, query * MEM_DEV + local, -1)
    req_ref[:, CAP:] = jnp.where(heads == HEADS, run[:, :128], starts[...]).astype(jnp.int32)


def route(lookups, block_slot):
    return pl.pallas_call(
        route_kernel,
        out_shape=[
            jax.ShapeDtypeStruct((DEVS, CAP + 128), jnp.int32),
            jax.ShapeDtypeStruct((TOK * HEADS * TOPK // ROWS, ROWS), jnp.int32),
        ],
        scratch_shapes=[
            pltpu.VMEM((TOK * HEADS * TOPK // ROWS, ROWS), jnp.int32),
            pltpu.VMEM((3 * DEVS, CAP), jnp.float32),
            pltpu.VMEM((CAP, BATCH * ROWS), jnp.bfloat16),
            pltpu.VMEM((3 * DEVS, BATCH * ROWS), jnp.bfloat16),
            pltpu.VMEM((DEVS, 128), jnp.float32),
        ],
        compiler_params=pltpu.CompilerParams(vmem_limit_bytes=32 * 1024 * 1024),
        cost_estimate=cost(22),
        name="route",
    )(lookups, block_slot.reshape(8, 128))


def turn_kernel(query_ref, out_ref):
    for h in range(HEADS):
        out_ref[h * TOK : (h + 1) * TOK, :] = query_ref[:, h * HEAD : (h + 1) * HEAD]


def turn(queries):
    return pl.pallas_call(
        turn_kernel,
        out_shape=jax.ShapeDtypeStruct((HEADS * TOK, HEAD), jnp.bfloat16),
        name="turn",
    )(queries)


def pick_rows(code_ref, start_ref, mem_ref, wanted, found, hot):
    @pl.when(pl.program_id(0) == 0)
    def _():
        wanted[CAP:, :] = jnp.full((WINDOW, GROUP), -1, jnp.int32)
        found[...] = jnp.zeros_like(found)

    for part in range(PARTS):
        span = slice(part * PART, (part + 1) * PART)
        code = jnp.transpose(code_ref[:, span])
        wanted[span, :] = (code & (MEM_DEV - 1)) + (code >> 16) * MEM_DEV
    row_ids = lax.broadcasted_iota(jnp.int32, (WINDOW, MEM_DEV), 1)
    for h in range(HEADS):
        begins = [start_ref[i, h] // 8 * 8 for i in range(GROUP)]
        most = start_ref[0, h + 1] - begins[0]
        for i in range(1, GROUP):
            most = jnp.maximum(most, start_ref[i, h + 1] - begins[i])

        def one_window(w, carry, h=h, begins=begins):
            for i in range(GROUP):
                at = pl.multiple_of(jnp.minimum(begins[i] + w * WINDOW, CAP), 8)
                col = wanted[pl.ds(at, WINDOW), i : i + 1] - h * MEM_DEV
                mine = slice(i * WINDOW, (i + 1) * WINDOW)
                hot[mine, :] = one_hot(col == row_ids)
                rows = jnp.dot(
                    hot[mine, :], mem_ref[:, h * HEAD : (h + 1) * HEAD], preferred_element_type=jnp.float32
                )
                own = (col[:8] >= 0) & (col[:8] < MEM_DEV)
                found[i, pl.ds(at, 8), :] = jnp.where(own, rows[:8], found[i, pl.ds(at, 8), :])
                found[i, pl.ds(at + 8, WINDOW - 8), :] = rows[8:]
            return carry

        lax.fori_loop(0, (most + WINDOW - 1) // WINDOW, one_window, 0)


PICK_SCRATCH = [
    pltpu.VMEM((CAP + WINDOW, GROUP), jnp.int32),
    pltpu.VMEM((GROUP, CAP + WINDOW, HEAD), jnp.float32),
    pltpu.VMEM((GROUP * WINDOW, MEM_DEV), jnp.bfloat16),
]
CODES = pl.BlockSpec((GROUP, CAP), lambda g: (g, 0))
STARTS = pl.BlockSpec((GROUP, 128), lambda g: (g, CAP // 128), memory_space=pltpu.SMEM)


def pick_kernel(code_ref, start_ref, value_ref, *refs):
    found = refs[PARTS + 1]
    pick_rows(code_ref, start_ref, value_ref, *refs[PARTS:])
    for i in range(GROUP):
        for part in range(PARTS):
            refs[part][i] = found[i, part * PART : (part + 1) * PART, :].astype(jnp.bfloat16)


def pick(codes, values):
    return pl.pallas_call(
        pick_kernel,
        grid=(DEVS // GROUP,),
        in_specs=[CODES, STARTS, pl.BlockSpec((MEM_DEV, HEADS * HEAD), lambda g: (0, 0))],
        out_specs=[pl.BlockSpec((GROUP, PART, HEAD), lambda g: (g, 0, 0))] * PARTS,
        out_shape=[jax.ShapeDtypeStruct((DEVS, PART, HEAD), jnp.bfloat16)] * PARTS,
        scratch_shapes=PICK_SCRATCH,
        compiler_params=pltpu.CompilerParams(vmem_limit_bytes=40 * 1024 * 1024),
        cost_estimate=cost(45),
        name="pick",
    )(codes, codes, values)


def score_kernel(code_ref, start_ref, key_ref, query_ref, *refs):
    out_ref, _, wanted, found, hot = refs[-5:]
    pick_rows(code_ref, start_ref, key_ref, wanted, found, hot)
    ids = lax.broadcasted_iota(jnp.int32, (HEADS * TOK, CAP), 0)
    for i in range(GROUP):
        keys = found[i, :CAP, :].astype(jnp.bfloat16)
        every = lax.dot_general(query_ref[i], keys, NT, preferred_element_type=jnp.float32)
        own = ids == code_ref[i : i + 1, :] >> 9
        out_ref[i : i + 1, :] = jnp.sum(jnp.where(own, every, 0.0), axis=0, keepdims=True) * HEAD ** (-0.5)


def score(codes, queries, keys, half, through, *ready):
    near = queries.shape[0] // GROUP
    steps = DEVS // GROUP // 2
    return pl.pallas_call(
        score_kernel,
        grid=(steps,),
        in_specs=[
            pl.BlockSpec((GROUP, CAP), lambda g: (g + half * steps, 0)),
            pl.BlockSpec((GROUP, 128), lambda g: (g + half * steps, CAP // 128), memory_space=pltpu.SMEM),
            pl.BlockSpec((MEM_DEV, HEADS * HEAD), lambda g: ((g + half * steps) // near, 0)),
            pl.BlockSpec((GROUP, HEADS * TOK, HEAD), lambda g: (g % near, 0, 0)),
            pl.BlockSpec(memory_space=pl.ANY),
        ]
        + [pl.BlockSpec(memory_space=pl.ANY)] * len(ready),
        out_specs=[CODES, pl.BlockSpec(memory_space=pl.ANY)],
        out_shape=[
            jax.ShapeDtypeStruct((DEVS // 2, CAP), jnp.float32),
            jax.ShapeDtypeStruct(through.shape, through.dtype),
        ],
        scratch_shapes=PICK_SCRATCH,
        input_output_aliases={4: 1},
        compiler_params=pltpu.CompilerParams(vmem_limit_bytes=40 * 1024 * 1024),
        cost_estimate=cost(40),
        name="score",
    )(codes, codes, keys, queries, through, *ready)


def join_kernel(a_ref, b_ref, _, out_ref):
    half = DEVS // 2
    out_ref[:half, :] = a_ref[...]
    out_ref[half:, :] = b_ref[...]


def join(one, two, ready):
    return pl.pallas_call(
        join_kernel,
        in_specs=[pl.BlockSpec(memory_space=pltpu.VMEM)] * 2 + [pl.BlockSpec(memory_space=pl.ANY)],
        out_shape=jax.ShapeDtypeStruct((DEVS, CAP), jnp.float32),
        name="join",
    )(one, two, ready)


def weigh_kernel(place_ref, score_ref, out_ref, parts, near, total, slots, spread):
    score = score_ref[...]
    for part in range(3):
        piece = score.astype(jnp.bfloat16)
        parts[part * DEVS : (part + 1) * DEVS, :] = piece
        score = score - piece.astype(jnp.float32)
    owners = lax.broadcasted_iota(jnp.int32, (DEVS, ROWS), 0)
    ranks = lax.broadcasted_iota(jnp.int32, (CAP, ROWS), 0)
    batches = place_ref.shape[0] // BATCH

    def fetch(i, carry):
        base = pl.multiple_of(i * BATCH, BATCH)
        place = place_ref[pl.ds(base, BATCH), :]
        rows = []
        for b in range(BATCH):
            here = place[b : b + 1, :]
            hot = one_hot(ranks == (here & (MEM_DEV - 1)))
            each = jnp.dot(parts[...], hot, preferred_element_type=jnp.float32)
            each = (each[:DEVS] + each[DEVS : 2 * DEVS]) + each[2 * DEVS :]
            rows.append(jnp.sum(jnp.where(owners == here // MEM_DEV, each, 0.0), axis=0, keepdims=True))
        near[pl.ds(base, BATCH), :] = jnp.concatenate(rows, axis=0)
        return carry

    lax.fori_loop(0, batches, fetch, 0)
    lane = lax.broadcasted_iota(jnp.int32, near.shape, 1)

    def across(x, op):
        for k in (16, 8, 4, 2, 1):
            other = jnp.where((lane & k) > 0, pltpu.roll(x, k, 1), pltpu.roll(x, ROWS - k, 1))
            x = op(x, other)
        return x

    score = near[...]
    power = jnp.exp(score - across(score, jnp.maximum))
    near[...] = power / across(power, jnp.add)
    total[...] = jnp.zeros_like(total)

    def scatter(i, carry):
        base = pl.multiple_of(i * BATCH, BATCH)
        place = place_ref[pl.ds(base, BATCH), :]
        prob = near[pl.ds(base, BATCH), :]
        for b in range(BATCH):
            here = place[b : b + 1, :]
            span = slice(b * ROWS, (b + 1) * ROWS)
            slots[:, span] = one_hot(ranks == (here & (MEM_DEV - 1)))
            mine = owners == here // MEM_DEV
            spread[:, span] = jnp.where(mine, prob[b : b + 1, :], 0.0).astype(jnp.bfloat16)
        total[...] += lax.dot_general(spread[...], slots[...], NT, preferred_element_type=jnp.float32)
        return carry

    lax.fori_loop(0, batches, scatter, 0)
    out_ref[...] = total[...]


def weigh(places, scores):
    return pl.pallas_call(
        weigh_kernel,
        out_shape=jax.ShapeDtypeStruct((DEVS, CAP), jnp.float32),
        scratch_shapes=[
            pltpu.VMEM((3 * DEVS, CAP), jnp.bfloat16),
            pltpu.VMEM(places.shape, jnp.float32),
            pltpu.VMEM((DEVS, CAP), jnp.float32),
            pltpu.VMEM((CAP, BATCH * ROWS), jnp.bfloat16),
            pltpu.VMEM((DEVS, BATCH * ROWS), jnp.bfloat16),
        ],
        compiler_params=pltpu.CompilerParams(vmem_limit_bytes=32 * 1024 * 1024),
        cost_estimate=cost(22),
        name="weigh",
    )(places, scores)


def mix_kernel(code_ref, weight_ref, value_ref, out_ref, spread):
    step = pl.program_id(0)

    @pl.when(step == 0)
    def _():
        out_ref[...] = jnp.zeros_like(out_ref)

    for i in range(GROUP):
        span = slice(i * PART, (i + 1) * PART)
        query = code_ref[i : i + 1, :] >> 9
        weight = weight_ref[i : i + 1, :]
        for h in range(HEADS):
            ids = lax.broadcasted_iota(jnp.int32, (TOK, PART), 0) + h * TOK
            spread[h * TOK : (h + 1) * TOK, span] = jnp.where(ids == query, weight, 0.0).astype(jnp.bfloat16)
    rows = value_ref[...].reshape(GROUP * PART, HEAD)
    for h in range(HEADS // 2):
        span = slice(h * 2 * TOK, (h + 1) * 2 * TOK)
        out_ref[span, :] += jnp.dot(spread[span, :], rows, preferred_element_type=jnp.float32)


def mix(codes, weights, values, part):
    return pl.pallas_call(
        mix_kernel,
        grid=(DEVS // GROUP,),
        in_specs=[
            pl.BlockSpec((GROUP, PART), lambda g: (g, part)),
            pl.BlockSpec((GROUP, PART), lambda g: (g, part)),
            pl.BlockSpec((GROUP, PART, HEAD), lambda g: (g, 0, 0)),
        ],
        out_specs=pl.BlockSpec((HEADS * TOK, HEAD), lambda g: (0, 0)),
        out_shape=jax.ShapeDtypeStruct((HEADS * TOK, HEAD), jnp.float32),
        scratch_shapes=[pltpu.VMEM((HEADS * TOK, GROUP * PART), jnp.bfloat16)],
        compiler_params=pltpu.CompilerParams(vmem_limit_bytes=32 * 1024 * 1024),
        cost_estimate=cost(15),
        name="mix",
    )(codes, weights, values)


def shards(queries, keys, values, mem_keys, mem_values, knn_index, block_slot, gate_bias, w_out):
    send = functools.partial(
        lax.all_to_all, axis_name=("seq", "mem"), split_axis=0, concat_axis=0, tiled=True
    )
    planes = lax.axis_size("seq")
    near = lax.axis_size("mem")
    near_queries = lax.all_gather(turn(queries[0]), "mem", axis=0, tiled=True).reshape(near, HEADS * TOK, HEAD)
    line_keys = lax.all_gather(mem_keys, "seq", axis=0, tiled=True)
    own = jnp.concatenate([keys[0], values[0]], axis=1)
    blocks = [own] + [
        lax.ppermute(own, "seq", [(i, i + back) for i in range(planes - back)]) for back in range(1, planes)
    ]

    lookups = knn_index[0].transpose(1, 0, 2).reshape(TOK * HEADS * TOPK // ROWS, ROWS)
    asked, places = route(lookups, block_slot)
    wanted = lax.all_to_all(
        asked.reshape(planes, near, CAP + 128), "mem", split_axis=1, concat_axis=1, tiled=True
    )
    codes = lax.all_to_all(wanted, "seq", split_axis=0, concat_axis=0, tiled=True).reshape(DEVS, CAP + 128)
    wanted = wanted.reshape(DEVS, CAP + 128)

    query = queries[0].reshape(TOK, HEADS, HEAD)
    seen = jnp.concatenate(blocks, axis=0)
    key_rows = seen[:, : HEADS * HEAD].reshape(-1, HEADS, HEAD)
    value_rows = seen[:, HEADS * HEAD :].reshape(-1, HEADS, HEAD)
    local = jnp.einsum("qhd,khd->hqk", query, key_rows, preferred_element_type=jnp.float32) * HEAD ** (-0.5)
    back = jnp.arange(seen.shape[0], dtype=jnp.int32) // TOK
    within = jnp.arange(seen.shape[0], dtype=jnp.int32) % TOK
    here = (back == 0)[None, :] & (within[None, :] <= jnp.arange(TOK, dtype=jnp.int32)[:, None])
    earlier = (back > 0) & (back <= lax.axis_index("seq"))
    local = jnp.where((here | earlier[None, :])[None], local, -jnp.inf)
    probs = jax.nn.softmax(local, axis=-1).astype(jnp.bfloat16)
    local_out = jnp.einsum("hqk,khd->hqd", probs, value_rows, preferred_element_type=jnp.float32)
    codes, local_out = lax.optimization_barrier((codes, local_out))

    picked = pick(codes, mem_values)
    first = send(picked[0])
    score_one, later = score(wanted, near_queries, line_keys, 0, picked[1])
    second = send(later)
    score_two, last = score(wanted, near_queries, line_keys, 1, picked[2], first)
    scored = join(score_one, score_two, second).reshape(planes, near, CAP)
    scores = lax.all_to_all(scored, "mem", split_axis=1, concat_axis=1, tiled=True).reshape(DEVS, CAP)
    third = send(last)
    weights = weigh(places, scores)
    sums = sum(mix(asked, weights, rows, part) for part, rows in enumerate((first, second, third)))
    mem_out = sums.reshape(HEADS, TOK, HEAD)

    gate = jax.nn.sigmoid(gate_bias)[:, None, None]
    combined = (gate * mem_out + (1.0 - gate) * local_out).astype(jnp.bfloat16)
    combined = combined.transpose(1, 0, 2).reshape(TOK, HEADS * HEAD)
    mixed = jnp.dot(combined, w_out, preferred_element_type=jnp.float32).astype(jnp.bfloat16)
    return mixed[None]


def solution(mesh):
    return jax.shard_map(
        shards,
        mesh=mesh,
        in_specs=(
            P("mem", "seq", None),
            P("mem", "seq", None),
            P("mem", "seq", None),
            P(("seq", "mem"), None),
            P(("seq", "mem"), None),
            P("mem", "seq", None, None),
            P(),
            P(),
            P(),
        ),
        out_specs=P("mem", "seq", None),
        check_vma=False,
    )
```

```python
import functools

import jax
import jax.numpy as jnp
from jax import lax
from jax.experimental import pallas as pl
from jax.experimental.pallas import tpu as pltpu
from jax.sharding import PartitionSpec as P

DEVS = 128
TOK = 128
HEADS = 8
HEAD = 128
TOPK = 32
MEM_DEV = 512
BLOCK = 64
CAP = 384
PART = 128
PARTS = CAP // PART
GROUP = 8
PICK = 16
BATCH = 8
ROWS = 256
WINDOW = 80
NT = (((1,), (1,)), ((), ()))


def one_hot(mask):
    return jnp.where(mask, 1.0, 0.0).astype(jnp.bfloat16)


def cost(micros):
    return pl.CostEstimate(flops=int(micros * 1e9), bytes_accessed=int(micros * 1e6), transcendentals=0)


def route_kernel(look_ref, slot_ref, req_ref, place_ref, store, total, slots, parts, starts):
    table = [jnp.broadcast_to(slot_ref[r : r + 1, :], (8, 128)) for r in range(8)]

    def translate(i, carry):
        base = pl.multiple_of(i * 8, 8)
        for half in range(ROWS // 128):
            look = look_ref[pl.ds(base, 8), half * 128 : (half + 1) * 128]
            blk = look >> 6
            low = blk & 127
            high = blk >> 7
            place = jnp.zeros((8, 128), jnp.int32)
            for r in range(8):
                place = jnp.where(high == r, jnp.take_along_axis(table[r], low, axis=1), place)
            store[pl.ds(base, 8), half * 128 : (half + 1) * 128] = place * BLOCK + (look & (BLOCK - 1))
        return carry

    lax.fori_loop(0, look_ref.shape[0] // 8, translate, 0)
    total[...] = jnp.zeros_like(total)
    starts[...] = jnp.zeros_like(starts)
    heads = lax.broadcasted_iota(jnp.int32, starts.shape, 1)
    upper = one_hot(
        lax.broadcasted_iota(jnp.int32, (ROWS, ROWS), 0) <= lax.broadcasted_iota(jnp.int32, (ROWS, ROWS), 1)
    )
    owners = lax.broadcasted_iota(jnp.int32, (DEVS, ROWS), 0)
    ranks = lax.broadcasted_iota(jnp.int32, (CAP, ROWS), 0)
    lane = lax.broadcasted_iota(jnp.int32, (1, ROWS), 1)
    batch = BATCH
    per_head = TOK * TOPK // ROWS

    def place(i, run):
        base = pl.multiple_of(i * batch, batch)
        rows = store[pl.ds(base, batch), :]
        starts[...] = jnp.where((heads * per_head == base) & (heads < HEADS), run[:, :128], starts[...])
        places = []
        for b in range(batch):
            row = base + b
            head = row // per_head
            tok = (row % per_head) * (ROWS // TOPK) + lane // TOPK
            here = rows[b : b + 1, :]
            owner = here // MEM_DEV
            mine = jnp.where(owners == owner, 1.0, 0.0)
            count = jnp.dot(mine.astype(jnp.bfloat16), upper, preferred_element_type=jnp.float32) + run
            rank = jnp.sum(mine * count, axis=0, keepdims=True).astype(jnp.int32) - 1
            run = jnp.broadcast_to(count[:, ROWS - 1 :], (DEVS, ROWS))
            places.append(owner * MEM_DEV + rank)
            span = slice(b * ROWS, (b + 1) * ROWS)
            slots[:, span] = one_hot(ranks == rank)
            local = here & (MEM_DEV - 1)
            first = (local & 255).astype(jnp.float32)
            second = ((local >> 8) + 2 * tok).astype(jnp.float32)
            parts[0:DEVS, span] = (mine * first).astype(jnp.bfloat16)
            parts[DEVS : 2 * DEVS, span] = (mine * second).astype(jnp.bfloat16)
            parts[2 * DEVS :, span] = (mine * (head + 1).astype(jnp.float32)).astype(jnp.bfloat16)
        total[...] += lax.dot_general(parts[...], slots[...], NT, preferred_element_type=jnp.float32)
        place_ref[pl.ds(base, batch), :] = jnp.concatenate(places, axis=0)
        return run

    run = lax.fori_loop(0, look_ref.shape[0] // batch, place, jnp.zeros((DEVS, ROWS), jnp.float32))
    first = total[0:DEVS, :].astype(jnp.int32)
    second = total[DEVS : 2 * DEVS, :].astype(jnp.int32)
    third = total[2 * DEVS :, :].astype(jnp.int32)
    local = first + (second & 1) * 256
    query = (third - 1) * TOK + (second >> 1)
    req_ref[:, :CAP] = jnp.where(third > 0, query * MEM_DEV + local, -1)
    req_ref[:, CAP:] = jnp.where(heads == HEADS, run[:, :128], starts[...]).astype(jnp.int32)


def route(lookups, block_slot):
    return pl.pallas_call(
        route_kernel,
        out_shape=[
            jax.ShapeDtypeStruct((DEVS, CAP + 128), jnp.int32),
            jax.ShapeDtypeStruct((TOK * HEADS * TOPK // ROWS, ROWS), jnp.int32),
        ],
        scratch_shapes=[
            pltpu.VMEM((TOK * HEADS * TOPK // ROWS, ROWS), jnp.int32),
            pltpu.VMEM((3 * DEVS, CAP), jnp.float32),
            pltpu.VMEM((CAP, BATCH * ROWS), jnp.bfloat16),
            pltpu.VMEM((3 * DEVS, BATCH * ROWS), jnp.bfloat16),
            pltpu.VMEM((DEVS, 128), jnp.float32),
        ],
        compiler_params=pltpu.CompilerParams(vmem_limit_bytes=32 * 1024 * 1024),
        cost_estimate=cost(22),
        name="route",
    )(lookups, block_slot.reshape(8, 128))


def turn_kernel(query_ref, out_ref):
    for h in range(HEADS):
        out_ref[h * TOK : (h + 1) * TOK, :] = query_ref[:, h * HEAD : (h + 1) * HEAD]


def turn(queries):
    return pl.pallas_call(
        turn_kernel,
        out_shape=jax.ShapeDtypeStruct((HEADS * TOK, HEAD), jnp.bfloat16),
        name="turn",
    )(queries)


def pick_rows(code_ref, start_ref, mem_ref, wanted, found, hot):
    group = code_ref.shape[0]

    @pl.when(pl.program_id(0) == 0)
    def _():
        wanted[CAP:, :] = jnp.full((WINDOW, group), -1.0, jnp.float32)
        found[...] = jnp.zeros_like(found)

    for part in range(PARTS):
        span = slice(part * PART, (part + 1) * PART)
        code = jnp.transpose(code_ref[:, span])
        wanted[span, :] = ((code & (MEM_DEV - 1)) + (code >> 16) * MEM_DEV).astype(jnp.float32)
    lanes = lax.broadcasted_iota(jnp.int32, (WINDOW, 128), 1).astype(jnp.float32)
    lane_ids = [lanes.astype(jnp.bfloat16), (lanes + 128).astype(jnp.bfloat16)]

    def product(h, spots, hot):
        for i, at in enumerate(spots):
            col = jnp.broadcast_to(wanted[pl.ds(at, WINDOW), i : i + 1], (WINDOW, 128))
            low = (col - h * MEM_DEV).astype(jnp.bfloat16)
            high = (col - (h * MEM_DEV + 256)).astype(jnp.bfloat16)
            for k, part in enumerate((low, low, high, high)):
                hot[i * WINDOW : (i + 1) * WINDOW, k * 128 : (k + 1) * 128] = jnp.where(
                    part == lane_ids[k % 2], jnp.bfloat16(1), jnp.bfloat16(0)
                )
        return jnp.dot(hot[...], mem_ref[:, h * HEAD : (h + 1) * HEAD], preferred_element_type=jnp.float32)

    def keep(h, i, at, rows):
        head = wanted[pl.ds(at, rows.shape[0]), i : i + 1]
        own = (head >= h * MEM_DEV) & (head < (h + 1) * MEM_DEV)
        found[i, pl.ds(at, rows.shape[0]), :] = jnp.where(own, rows, found[i, pl.ds(at, rows.shape[0]), :])

    begins = [[start_ref[i, h] // 8 * 8 for i in range(group)] for h in range(HEADS)]
    for h in range(HEADS):
        spots = [pl.multiple_of(at, 8) for at in begins[h]]
        rows = product(h, spots, hot.at[h % 2])
        for i, at in enumerate(spots):
            mine = rows[i * WINDOW : (i + 1) * WINDOW]
            keep(h, i, at, mine[:8])
            found[i, pl.ds(at + 8, WINDOW - 8), :] = mine[8:]

    for h in range(HEADS):
        most = start_ref[0, h + 1] - begins[h][0]
        for i in range(1, group):
            most = jnp.maximum(most, start_ref[i, h + 1] - begins[h][i])

        def one_window(w, carry, h=h):
            spots = [pl.multiple_of(jnp.minimum(at + w * WINDOW, CAP), 8) for at in begins[h]]
            rows = product(h, spots, hot.at[0])
            for i, at in enumerate(spots):
                keep(h, i, at, rows[i * WINDOW : (i + 1) * WINDOW])
            return carry

        lax.fori_loop(1, (most + WINDOW - 1) // WINDOW, one_window, 0)


def pick_specs(group):
    specs = [
        pl.BlockSpec((group, CAP), lambda g: (g, 0)),
        pl.BlockSpec((group, 128), lambda g: (g, CAP // 128), memory_space=pltpu.SMEM),
    ]
    scratch = [
        pltpu.VMEM((CAP + WINDOW, group), jnp.float32),
        pltpu.VMEM((group, CAP + WINDOW, HEAD), jnp.float32),
        pltpu.VMEM((2, group * WINDOW, MEM_DEV), jnp.bfloat16),
    ]
    return specs, scratch


def pick_kernel(code_ref, start_ref, value_ref, first_ref, last_ref, wanted, found, hot):
    pick_rows(code_ref, start_ref, value_ref, wanted, found, hot)
    for i in range(code_ref.shape[0]):
        first_ref[i] = found[i, : CAP - PART, :].astype(jnp.bfloat16)
        last_ref[i] = found[i, CAP - PART : CAP, :].astype(jnp.bfloat16)


def pick(codes, values):
    specs, scratch = pick_specs(PICK)
    sizes = (CAP - PART, PART)
    return pl.pallas_call(
        pick_kernel,
        grid=(DEVS // PICK,),
        in_specs=specs + [pl.BlockSpec((MEM_DEV, HEADS * HEAD), lambda g: (0, 0))],
        out_specs=[pl.BlockSpec((PICK, size, HEAD), lambda g: (g, 0, 0)) for size in sizes],
        out_shape=[pltpu.HBM((DEVS, size, HEAD), jnp.bfloat16) for size in sizes],
        scratch_shapes=scratch,
        compiler_params=pltpu.CompilerParams(vmem_limit_bytes=40 * 1024 * 1024),
        cost_estimate=cost(40),
        name="pick",
    )(codes, codes, values)


def score_kernel(code_ref, start_ref, key_ref, query_ref, _, out_ref, __, wanted, found, hot):
    pick_rows(code_ref, start_ref, key_ref, wanted, found, hot)
    ids = lax.broadcasted_iota(jnp.int32, (HEADS * TOK, CAP), 0)
    for i in range(GROUP):
        keys = found[i, :CAP, :].astype(jnp.bfloat16)
        every = lax.dot_general(query_ref[i], keys, NT, preferred_element_type=jnp.float32)
        own = ids == code_ref[i : i + 1, :] >> 9
        out_ref[i : i + 1, :] = jnp.sum(jnp.where(own, every, 0.0), axis=0, keepdims=True) * HEAD ** (-0.5)


def score(codes, queries, keys, through):
    near = queries.shape[0] // GROUP
    specs, scratch = pick_specs(GROUP)
    return pl.pallas_call(
        score_kernel,
        grid=(DEVS // GROUP,),
        in_specs=specs
        + [
            pl.BlockSpec((MEM_DEV, HEADS * HEAD), lambda g: (g // near, 0)),
            pl.BlockSpec((GROUP, HEADS * TOK, HEAD), lambda g: (g % near, 0, 0)),
            pl.BlockSpec(memory_space=pl.ANY),
        ],
        out_specs=[specs[0], pl.BlockSpec(memory_space=pl.ANY)],
        out_shape=[
            jax.ShapeDtypeStruct((DEVS, CAP), jnp.float32),
            jax.ShapeDtypeStruct(through.shape, through.dtype),
        ],
        scratch_shapes=scratch,
        input_output_aliases={4: 1},
        compiler_params=pltpu.CompilerParams(vmem_limit_bytes=40 * 1024 * 1024),
        cost_estimate=cost(75),
        name="score",
    )(codes, codes, keys, queries, through)


def join_kernel(a_ref, _, __, out_ref):
    out_ref[...] = a_ref[...]


def join(scores, *ready):
    return pl.pallas_call(
        join_kernel,
        in_specs=[pl.BlockSpec(memory_space=pltpu.VMEM)] + [pl.BlockSpec(memory_space=pl.ANY)] * len(ready),
        out_shape=jax.ShapeDtypeStruct(scores.shape, scores.dtype),
        name="join",
    )(scores, *ready)


def weigh_kernel(place_ref, score_ref, out_ref, parts, near, total, slots, spread):
    score = score_ref[...]
    for part in range(3):
        piece = score.astype(jnp.bfloat16)
        parts[part * DEVS : (part + 1) * DEVS, :] = piece
        score = score - piece.astype(jnp.float32)
    owners = lax.broadcasted_iota(jnp.int32, (DEVS, ROWS), 0)
    ranks = lax.broadcasted_iota(jnp.int32, (CAP, ROWS), 0)
    batches = place_ref.shape[0] // BATCH

    def fetch(i, carry):
        base = pl.multiple_of(i * BATCH, BATCH)
        place = place_ref[pl.ds(base, BATCH), :]
        rows = []
        for b in range(BATCH):
            here = place[b : b + 1, :]
            hot = one_hot(ranks == (here & (MEM_DEV - 1)))
            each = jnp.dot(parts[...], hot, preferred_element_type=jnp.float32)
            each = (each[:DEVS] + each[DEVS : 2 * DEVS]) + each[2 * DEVS :]
            rows.append(jnp.sum(jnp.where(owners == here // MEM_DEV, each, 0.0), axis=0, keepdims=True))
        near[pl.ds(base, BATCH), :] = jnp.concatenate(rows, axis=0)
        return carry

    lax.fori_loop(0, batches, fetch, 0)
    lane = lax.broadcasted_iota(jnp.int32, near.shape, 1)

    def across(x, op):
        for k in (16, 8, 4, 2, 1):
            other = jnp.where((lane & k) > 0, pltpu.roll(x, k, 1), pltpu.roll(x, ROWS - k, 1))
            x = op(x, other)
        return x

    score = near[...]
    power = jnp.exp(score - across(score, jnp.maximum))
    near[...] = power / across(power, jnp.add)
    total[...] = jnp.zeros_like(total)

    def scatter(i, carry):
        base = pl.multiple_of(i * BATCH, BATCH)
        place = place_ref[pl.ds(base, BATCH), :]
        prob = near[pl.ds(base, BATCH), :]
        for b in range(BATCH):
            here = place[b : b + 1, :]
            span = slice(b * ROWS, (b + 1) * ROWS)
            slots[:, span] = one_hot(ranks == (here & (MEM_DEV - 1)))
            mine = owners == here // MEM_DEV
            spread[:, span] = jnp.where(mine, prob[b : b + 1, :], 0.0).astype(jnp.bfloat16)
        total[...] += lax.dot_general(spread[...], slots[...], NT, preferred_element_type=jnp.float32)
        return carry

    lax.fori_loop(0, batches, scatter, 0)
    out_ref[...] = total[...]


def weigh(places, scores):
    return pl.pallas_call(
        weigh_kernel,
        out_shape=jax.ShapeDtypeStruct((DEVS, CAP), jnp.float32),
        scratch_shapes=[
            pltpu.VMEM((3 * DEVS, CAP), jnp.bfloat16),
            pltpu.VMEM(places.shape, jnp.float32),
            pltpu.VMEM((DEVS, CAP), jnp.float32),
            pltpu.VMEM((CAP, BATCH * ROWS), jnp.bfloat16),
            pltpu.VMEM((DEVS, BATCH * ROWS), jnp.bfloat16),
        ],
        compiler_params=pltpu.CompilerParams(vmem_limit_bytes=32 * 1024 * 1024),
        cost_estimate=cost(22),
        name="weigh",
    )(places, scores)


def mix_kernel(code_ref, start_ref, weight_ref, value_ref, out_ref, spread, rows, *, begin):
    part = pl.program_id(1)
    half = HEADS // 2

    @pl.when((pl.program_id(0) == 0) & (part == 0))
    def _():
        out_ref[...] = jnp.zeros_like(out_ref)

    slot = lax.broadcasted_iota(jnp.int32, (PART, HEAD), 0).astype(jnp.float32).astype(jnp.bfloat16)
    for i in range(GROUP):
        span = slice(i * PART, (i + 1) * PART)
        first = jnp.clip(start_ref[i, half] - (begin + part) * PART, 0, PART)
        later = slot >= first.astype(jnp.float32).astype(jnp.bfloat16)
        value = value_ref[i]
        rows[span, :HEAD] = jnp.where(later, jnp.bfloat16(0), value)
        rows[span, HEAD:] = jnp.where(later, value, jnp.bfloat16(0))
        query = (code_ref[i : i + 1, :] >> 9) & (half * TOK - 1)
        weight = weight_ref[i : i + 1, :]
        for h in range(half):
            ids = lax.broadcasted_iota(jnp.int32, (TOK, PART), 0) + h * TOK
            spread[h * TOK : (h + 1) * TOK, span] = jnp.where(ids == query, weight, 0.0).astype(jnp.bfloat16)
    out_ref[...] += jnp.dot(spread[...], rows[...], preferred_element_type=jnp.float32)


def mix(codes, weights, values, begin):
    parts = values.shape[1] // PART
    return pl.pallas_call(
        functools.partial(mix_kernel, begin=begin),
        grid=(DEVS // GROUP, parts),
        in_specs=[
            pl.BlockSpec((GROUP, PART), lambda g, p: (g, begin + p)),
            pl.BlockSpec((GROUP, 128), lambda g, p: (g, CAP // 128), memory_space=pltpu.SMEM),
            pl.BlockSpec((GROUP, PART), lambda g, p: (g, begin + p)),
            pl.BlockSpec((GROUP, PART, HEAD), lambda g, p: (g, p, 0)),
        ],
        out_specs=pl.BlockSpec((HEADS // 2 * TOK, 2 * HEAD), lambda g, p: (0, 0)),
        out_shape=jax.ShapeDtypeStruct((HEADS // 2 * TOK, 2 * HEAD), jnp.float32),
        scratch_shapes=[
            pltpu.VMEM((HEADS // 2 * TOK, GROUP * PART), jnp.bfloat16),
            pltpu.VMEM((GROUP * PART, 2 * HEAD), jnp.bfloat16),
        ],
        compiler_params=pltpu.CompilerParams(vmem_limit_bytes=32 * 1024 * 1024),
        cost_estimate=cost(12 * parts),
        name="mix",
    )(codes, codes, weights, values)


def shards(queries, keys, values, mem_keys, mem_values, knn_index, block_slot, gate_bias, w_out):
    send = functools.partial(
        lax.all_to_all, axis_name=("seq", "mem"), split_axis=0, concat_axis=0, tiled=True
    )
    planes = lax.axis_size("seq")
    near = lax.axis_size("mem")
    near_queries = lax.all_gather(turn(queries[0]), "mem", axis=0, tiled=True).reshape(near, HEADS * TOK, HEAD)
    line_keys = lax.all_gather(mem_keys, "seq", axis=0, tiled=True)
    own = jnp.concatenate([keys[0], values[0]], axis=1)
    blocks = [own] + [
        lax.ppermute(own, "seq", [(i, i + back) for i in range(planes - back)]) for back in range(1, planes)
    ]

    lookups = knn_index[0].transpose(1, 0, 2).reshape(TOK * HEADS * TOPK // ROWS, ROWS)
    asked, places = route(lookups, block_slot)
    wanted = lax.all_to_all(
        asked.reshape(planes, near, CAP + 128), "mem", split_axis=1, concat_axis=1, tiled=True
    )
    codes = lax.all_to_all(wanted, "seq", split_axis=0, concat_axis=0, tiled=True).reshape(DEVS, CAP + 128)
    wanted = wanted.reshape(DEVS, CAP + 128)

    query = queries[0].reshape(TOK, HEADS, HEAD)
    seen = jnp.concatenate(blocks, axis=0)
    key_rows = seen[:, : HEADS * HEAD].reshape(-1, HEADS, HEAD)
    value_rows = seen[:, HEADS * HEAD :].reshape(-1, HEADS, HEAD)
    local = jnp.einsum("qhd,khd->hqk", query, key_rows, preferred_element_type=jnp.float32) * HEAD ** (-0.5)
    back = jnp.arange(seen.shape[0], dtype=jnp.int32) // TOK
    within = jnp.arange(seen.shape[0], dtype=jnp.int32) % TOK
    here = (back == 0)[None, :] & (within[None, :] <= jnp.arange(TOK, dtype=jnp.int32)[:, None])
    earlier = (back > 0) & (back <= lax.axis_index("seq"))
    local = jnp.where((here | earlier[None, :])[None], local, -jnp.inf)
    probs = jax.nn.softmax(local, axis=-1).astype(jnp.bfloat16)
    local_out = jnp.einsum("hqk,khd->hqd", probs, value_rows, preferred_element_type=jnp.float32)
    picked, later = pick(codes, mem_values)
    first = send(picked)
    scored, later = score(wanted, near_queries, line_keys, later)
    scored = join(scored, first, local_out).reshape(planes, near, CAP)
    scores = lax.all_to_all(scored, "mem", split_axis=1, concat_axis=1, tiled=True).reshape(DEVS, CAP)
    last = send(later)
    weights = weigh(places, scores)
    sums = mix(asked, weights, first, 0) + mix(asked, weights, last, PARTS - 1)
    mem_out = jnp.concatenate([sums[:, :HEAD], sums[:, HEAD:]], axis=0).reshape(HEADS, TOK, HEAD)

    gate = jax.nn.sigmoid(gate_bias)[:, None, None]
    combined = (gate * mem_out + (1.0 - gate) * local_out).astype(jnp.bfloat16)
    combined = combined.transpose(1, 0, 2).reshape(TOK, HEADS * HEAD)
    mixed = jnp.dot(combined, w_out, preferred_element_type=jnp.float32).astype(jnp.bfloat16)
    return mixed[None]


def solution(mesh):
    return jax.shard_map(
        shards,
        mesh=mesh,
        in_specs=(
            P("mem", "seq", None),
            P("mem", "seq", None),
            P("mem", "seq", None),
            P(("seq", "mem"), None),
            P(("seq", "mem"), None),
            P("mem", "seq", None, None),
            P(),
            P(),
            P(),
        ),
        out_specs=P("mem", "seq", None),
        check_vma=False,
    )
```

```python
import functools

import jax
import jax.numpy as jnp
from jax import lax
from jax.experimental import pallas as pl
from jax.experimental.pallas import tpu as pltpu
from jax.sharding import PartitionSpec as P

DEVS = 128
TOK = 128
HEADS = 8
HEAD = 128
TOPK = 32
MEM_DEV = 512
BLOCK = 64
CAP = 384
PART = 128
PARTS = CAP // PART
GROUP = 8
PICK = 16
BATCH = 8
ROWS = 256
WINDOW = 80
NT = (((1,), (1,)), ((), ()))


def one_hot(mask):
    return jnp.where(mask, 1.0, 0.0).astype(jnp.bfloat16)


def cost(micros):
    return pl.CostEstimate(flops=int(micros * 1e9), bytes_accessed=int(micros * 1e6), transcendentals=0)


def route_kernel(look_ref, slot_ref, req_ref, place_ref, store, total, slots, parts, starts):
    table = [jnp.broadcast_to(slot_ref[r : r + 1, :], (8, 128)) for r in range(8)]

    def translate(i, carry):
        base = pl.multiple_of(i * 8, 8)
        for half in range(ROWS // 128):
            look = look_ref[pl.ds(base, 8), half * 128 : (half + 1) * 128]
            blk = look >> 6
            low = blk & 127
            high = blk >> 7
            place = jnp.zeros((8, 128), jnp.int32)
            for r in range(8):
                place = jnp.where(high == r, jnp.take_along_axis(table[r], low, axis=1), place)
            store[pl.ds(base, 8), half * 128 : (half + 1) * 128] = place * BLOCK + (look & (BLOCK - 1))
        return carry

    lax.fori_loop(0, look_ref.shape[0] // 8, translate, 0)
    total[...] = jnp.zeros_like(total)
    starts[...] = jnp.zeros_like(starts)
    heads = lax.broadcasted_iota(jnp.int32, starts.shape, 1)
    upper = one_hot(
        lax.broadcasted_iota(jnp.int32, (ROWS, ROWS), 0) <= lax.broadcasted_iota(jnp.int32, (ROWS, ROWS), 1)
    )
    owners = lax.broadcasted_iota(jnp.int32, (DEVS, ROWS), 0)
    ranks = lax.broadcasted_iota(jnp.int32, (CAP, ROWS), 0)
    lane = lax.broadcasted_iota(jnp.int32, (1, ROWS), 1)
    batch = BATCH
    per_head = TOK * TOPK // ROWS

    def place(i, run):
        base = pl.multiple_of(i * batch, batch)
        rows = store[pl.ds(base, batch), :]
        starts[...] = jnp.where((heads * per_head == base) & (heads < HEADS), run[:, :128], starts[...])
        places = []
        for b in range(batch):
            row = base + b
            head = row // per_head
            tok = (row % per_head) * (ROWS // TOPK) + lane // TOPK
            here = rows[b : b + 1, :]
            owner = here // MEM_DEV
            mine = jnp.where(owners == owner, 1.0, 0.0)
            count = jnp.dot(mine.astype(jnp.bfloat16), upper, preferred_element_type=jnp.float32) + run
            rank = jnp.sum(mine * count, axis=0, keepdims=True).astype(jnp.int32) - 1
            run = jnp.broadcast_to(count[:, ROWS - 1 :], (DEVS, ROWS))
            places.append(owner * MEM_DEV + rank)
            span = slice(b * ROWS, (b + 1) * ROWS)
            slots[:, span] = one_hot(ranks == rank)
            local = here & (MEM_DEV - 1)
            first = (local & 255).astype(jnp.float32)
            second = ((local >> 8) + 2 * tok).astype(jnp.float32)
            parts[0:DEVS, span] = (mine * first).astype(jnp.bfloat16)
            parts[DEVS : 2 * DEVS, span] = (mine * second).astype(jnp.bfloat16)
            parts[2 * DEVS :, span] = (mine * (head + 1).astype(jnp.float32)).astype(jnp.bfloat16)
        total[...] += lax.dot_general(parts[...], slots[...], NT, preferred_element_type=jnp.float32)
        place_ref[pl.ds(base, batch), :] = jnp.concatenate(places, axis=0)
        return run

    run = lax.fori_loop(0, look_ref.shape[0] // batch, place, jnp.zeros((DEVS, ROWS), jnp.float32))
    first = total[0:DEVS, :].astype(jnp.int32)
    second = total[DEVS : 2 * DEVS, :].astype(jnp.int32)
    third = total[2 * DEVS :, :].astype(jnp.int32)
    local = first + (second & 1) * 256
    query = (third - 1) * TOK + (second >> 1)
    req_ref[:, :CAP] = jnp.where(third > 0, query * MEM_DEV + local, -1)
    req_ref[:, CAP:] = jnp.where(heads == HEADS, run[:, :128], starts[...]).astype(jnp.int32)


def route(lookups, block_slot):
    return pl.pallas_call(
        route_kernel,
        out_shape=[
            jax.ShapeDtypeStruct((DEVS, CAP + 128), jnp.int32),
            jax.ShapeDtypeStruct((TOK * HEADS * TOPK // ROWS, ROWS), jnp.int32),
        ],
        scratch_shapes=[
            pltpu.VMEM((TOK * HEADS * TOPK // ROWS, ROWS), jnp.int32),
            pltpu.VMEM((3 * DEVS, CAP), jnp.float32),
            pltpu.VMEM((CAP, BATCH * ROWS), jnp.bfloat16),
            pltpu.VMEM((3 * DEVS, BATCH * ROWS), jnp.bfloat16),
            pltpu.VMEM((DEVS, 128), jnp.float32),
        ],
        compiler_params=pltpu.CompilerParams(vmem_limit_bytes=32 * 1024 * 1024),
        cost_estimate=cost(22),
        name="route",
    )(lookups, block_slot.reshape(8, 128))


def turn_kernel(query_ref, out_ref):
    for h in range(HEADS):
        out_ref[h * TOK : (h + 1) * TOK, :] = query_ref[:, h * HEAD : (h + 1) * HEAD]


def turn(queries):
    return pl.pallas_call(
        turn_kernel,
        out_shape=jax.ShapeDtypeStruct((HEADS * TOK, HEAD), jnp.bfloat16),
        name="turn",
    )(queries)


def pick_rows(code_ref, start_ref, mem_ref, wanted, found, hot):
    group = code_ref.shape[0]

    @pl.when(pl.program_id(0) == 0)
    def _():
        wanted[CAP:, :] = jnp.full((WINDOW, group), -1.0, jnp.float32)
        found[...] = jnp.zeros_like(found)

    for part in range(PARTS):
        span = slice(part * PART, (part + 1) * PART)
        code = jnp.transpose(code_ref[:, span])
        wanted[span, :] = ((code & (MEM_DEV - 1)) + (code >> 16) * MEM_DEV).astype(jnp.float32)
    lanes = lax.broadcasted_iota(jnp.int32, (WINDOW, 128), 1).astype(jnp.float32)
    lane_ids = [lanes.astype(jnp.bfloat16), (lanes + 128).astype(jnp.bfloat16)]

    def product(h, spots, hot):
        for i, at in enumerate(spots):
            col = jnp.broadcast_to(wanted[pl.ds(at, WINDOW), i : i + 1], (WINDOW, 128))
            low = (col - h * MEM_DEV).astype(jnp.bfloat16)
            high = (col - (h * MEM_DEV + 256)).astype(jnp.bfloat16)
            for k, part in enumerate((low, low, high, high)):
                hot[i * WINDOW : (i + 1) * WINDOW, k * 128 : (k + 1) * 128] = jnp.where(
                    part == lane_ids[k % 2], jnp.bfloat16(1), jnp.bfloat16(0)
                )
        return jnp.dot(hot[...], mem_ref[:, h * HEAD : (h + 1) * HEAD], preferred_element_type=jnp.float32)

    def keep(h, i, at, rows):
        head = wanted[pl.ds(at, rows.shape[0]), i : i + 1]
        own = (head >= h * MEM_DEV) & (head < (h + 1) * MEM_DEV)
        found[i, pl.ds(at, rows.shape[0]), :] = jnp.where(own, rows, found[i, pl.ds(at, rows.shape[0]), :])

    begins = [[start_ref[i, h] // 8 * 8 for i in range(group)] for h in range(HEADS)]
    for h in range(HEADS):
        spots = [pl.multiple_of(at, 8) for at in begins[h]]
        rows = product(h, spots, hot.at[h % 2])
        for i, at in enumerate(spots):
            mine = rows[i * WINDOW : (i + 1) * WINDOW]
            keep(h, i, at, mine[:8])
            found[i, pl.ds(at + 8, WINDOW - 8), :] = mine[8:]

    for h in range(HEADS):
        most = start_ref[0, h + 1] - begins[h][0]
        for i in range(1, group):
            most = jnp.maximum(most, start_ref[i, h + 1] - begins[h][i])

        def one_window(w, carry, h=h):
            spots = [pl.multiple_of(jnp.minimum(at + w * WINDOW, CAP), 8) for at in begins[h]]
            rows = product(h, spots, hot.at[0])
            for i, at in enumerate(spots):
                keep(h, i, at, rows[i * WINDOW : (i + 1) * WINDOW])
            return carry

        lax.fori_loop(1, (most + WINDOW - 1) // WINDOW, one_window, 0)


def pick_specs(group):
    specs = [
        pl.BlockSpec((group, CAP), lambda g: (g, 0)),
        pl.BlockSpec((group, 128), lambda g: (g, CAP // 128), memory_space=pltpu.SMEM),
    ]
    scratch = [
        pltpu.VMEM((CAP + WINDOW, group), jnp.float32),
        pltpu.VMEM((group, CAP + WINDOW, HEAD), jnp.float32),
        pltpu.VMEM((2, group * WINDOW, MEM_DEV), jnp.bfloat16),
    ]
    return specs, scratch


def pick_kernel(code_ref, start_ref, value_ref, _, first_ref, last_ref, wanted, found, hot):
    pick_rows(code_ref, start_ref, value_ref, wanted, found, hot)
    for i in range(code_ref.shape[0]):
        first_ref[i] = found[i, : CAP - PART, :].astype(jnp.bfloat16)
        last_ref[i] = found[i, CAP - PART : CAP, :].astype(jnp.bfloat16)


def pick(codes, values, ready):
    specs, scratch = pick_specs(PICK)
    sizes = (CAP - PART, PART)
    return pl.pallas_call(
        pick_kernel,
        grid=(DEVS // PICK,),
        in_specs=specs
        + [pl.BlockSpec((MEM_DEV, HEADS * HEAD), lambda g: (0, 0)), pl.BlockSpec(memory_space=pl.ANY)],
        out_specs=[pl.BlockSpec((PICK, size, HEAD), lambda g: (g, 0, 0)) for size in sizes],
        out_shape=[pltpu.HBM((DEVS, size, HEAD), jnp.bfloat16) for size in sizes],
        scratch_shapes=scratch,
        compiler_params=pltpu.CompilerParams(vmem_limit_bytes=40 * 1024 * 1024),
        cost_estimate=cost(40),
        name="pick",
    )(codes, codes, values, ready)


def score_kernel(code_ref, start_ref, key_ref, query_ref, _, out_ref, __, wanted, found, hot):
    pick_rows(code_ref, start_ref, key_ref, wanted, found, hot)
    ids = lax.broadcasted_iota(jnp.int32, (HEADS * TOK, CAP), 0)
    for i in range(GROUP):
        keys = found[i, :CAP, :].astype(jnp.bfloat16)
        every = lax.dot_general(query_ref[i], keys, NT, preferred_element_type=jnp.float32)
        own = ids == code_ref[i : i + 1, :] >> 9
        out_ref[i : i + 1, :] = jnp.sum(jnp.where(own, every, 0.0), axis=0, keepdims=True) * HEAD ** (-0.5)


def score(codes, queries, keys, through):
    near = queries.shape[0] // GROUP
    specs, scratch = pick_specs(GROUP)
    return pl.pallas_call(
        score_kernel,
        grid=(DEVS // GROUP,),
        in_specs=specs
        + [
            pl.BlockSpec((MEM_DEV, HEADS * HEAD), lambda g: (g // near, 0)),
            pl.BlockSpec((GROUP, HEADS * TOK, HEAD), lambda g: (g % near, 0, 0)),
            pl.BlockSpec(memory_space=pl.ANY),
        ],
        out_specs=[specs[0], pl.BlockSpec(memory_space=pl.ANY)],
        out_shape=[
            jax.ShapeDtypeStruct((DEVS, CAP), jnp.float32),
            jax.ShapeDtypeStruct(through.shape, through.dtype),
        ],
        scratch_shapes=scratch,
        input_output_aliases={4: 1},
        compiler_params=pltpu.CompilerParams(vmem_limit_bytes=40 * 1024 * 1024),
        cost_estimate=cost(75),
        name="score",
    )(codes, codes, keys, queries, through)


def join_kernel(a_ref, _, out_ref):
    out_ref[...] = a_ref[...]


def join(scores, ready):
    return pl.pallas_call(
        join_kernel,
        in_specs=[pl.BlockSpec(memory_space=pltpu.VMEM)] + [pl.BlockSpec(memory_space=pl.ANY)],
        out_shape=jax.ShapeDtypeStruct(scores.shape, scores.dtype),
        name="join",
    )(scores, ready)


def weigh_kernel(place_ref, score_ref, out_ref, parts, near, total, slots, spread):
    score = score_ref[...]
    for part in range(3):
        piece = score.astype(jnp.bfloat16)
        parts[part * DEVS : (part + 1) * DEVS, :] = piece
        score = score - piece.astype(jnp.float32)
    owners = lax.broadcasted_iota(jnp.int32, (DEVS, ROWS), 0)
    ranks = lax.broadcasted_iota(jnp.int32, (CAP, ROWS), 0)
    batches = place_ref.shape[0] // BATCH

    def fetch(i, carry):
        base = pl.multiple_of(i * BATCH, BATCH)
        place = place_ref[pl.ds(base, BATCH), :]
        rows = []
        for b in range(BATCH):
            here = place[b : b + 1, :]
            hot = one_hot(ranks == (here & (MEM_DEV - 1)))
            each = jnp.dot(parts[...], hot, preferred_element_type=jnp.float32)
            each = (each[:DEVS] + each[DEVS : 2 * DEVS]) + each[2 * DEVS :]
            rows.append(jnp.sum(jnp.where(owners == here // MEM_DEV, each, 0.0), axis=0, keepdims=True))
        near[pl.ds(base, BATCH), :] = jnp.concatenate(rows, axis=0)
        return carry

    lax.fori_loop(0, batches, fetch, 0)
    lane = lax.broadcasted_iota(jnp.int32, near.shape, 1)

    def across(x, op):
        for k in (16, 8, 4, 2, 1):
            other = jnp.where((lane & k) > 0, pltpu.roll(x, k, 1), pltpu.roll(x, ROWS - k, 1))
            x = op(x, other)
        return x

    score = near[...]
    power = jnp.exp(score - across(score, jnp.maximum))
    near[...] = power / across(power, jnp.add)
    total[...] = jnp.zeros_like(total)

    def scatter(i, carry):
        base = pl.multiple_of(i * BATCH, BATCH)
        place = place_ref[pl.ds(base, BATCH), :]
        prob = near[pl.ds(base, BATCH), :]
        for b in range(BATCH):
            here = place[b : b + 1, :]
            span = slice(b * ROWS, (b + 1) * ROWS)
            slots[:, span] = one_hot(ranks == (here & (MEM_DEV - 1)))
            mine = owners == here // MEM_DEV
            spread[:, span] = jnp.where(mine, prob[b : b + 1, :], 0.0).astype(jnp.bfloat16)
        total[...] += lax.dot_general(spread[...], slots[...], NT, preferred_element_type=jnp.float32)
        return carry

    lax.fori_loop(0, batches, scatter, 0)
    out_ref[...] = total[...]


def weigh(places, scores):
    return pl.pallas_call(
        weigh_kernel,
        out_shape=jax.ShapeDtypeStruct((DEVS, CAP), jnp.float32),
        scratch_shapes=[
            pltpu.VMEM((3 * DEVS, CAP), jnp.bfloat16),
            pltpu.VMEM(places.shape, jnp.float32),
            pltpu.VMEM((DEVS, CAP), jnp.float32),
            pltpu.VMEM((CAP, BATCH * ROWS), jnp.bfloat16),
            pltpu.VMEM((DEVS, BATCH * ROWS), jnp.bfloat16),
        ],
        compiler_params=pltpu.CompilerParams(vmem_limit_bytes=32 * 1024 * 1024),
        cost_estimate=cost(22),
        name="weigh",
    )(places, scores)


def mix_kernel(code_ref, start_ref, weight_ref, value_ref, out_ref, spread, rows, *, begin):
    part = pl.program_id(1)
    half = HEADS // 2

    @pl.when((pl.program_id(0) == 0) & (part == 0))
    def _():
        out_ref[...] = jnp.zeros_like(out_ref)

    slot = lax.broadcasted_iota(jnp.int32, (PART, HEAD), 0).astype(jnp.float32).astype(jnp.bfloat16)
    for i in range(GROUP):
        span = slice(i * PART, (i + 1) * PART)
        first = jnp.clip(start_ref[i, half] - (begin + part) * PART, 0, PART)
        later = slot >= first.astype(jnp.float32).astype(jnp.bfloat16)
        value = value_ref[i]
        rows[span, :HEAD] = jnp.where(later, jnp.bfloat16(0), value)
        rows[span, HEAD:] = jnp.where(later, value, jnp.bfloat16(0))
        query = (code_ref[i : i + 1, :] >> 9) & (half * TOK - 1)
        weight = weight_ref[i : i + 1, :]
        for h in range(half):
            ids = lax.broadcasted_iota(jnp.int32, (TOK, PART), 0) + h * TOK
            spread[h * TOK : (h + 1) * TOK, span] = jnp.where(ids == query, weight, 0.0).astype(jnp.bfloat16)
    out_ref[...] += jnp.dot(spread[...], rows[...], preferred_element_type=jnp.float32)


def mix(codes, weights, values, begin):
    parts = values.shape[1] // PART
    return pl.pallas_call(
        functools.partial(mix_kernel, begin=begin),
        grid=(DEVS // GROUP, parts),
        in_specs=[
            pl.BlockSpec((GROUP, PART), lambda g, p: (g, begin + p)),
            pl.BlockSpec((GROUP, 128), lambda g, p: (g, CAP // 128), memory_space=pltpu.SMEM),
            pl.BlockSpec((GROUP, PART), lambda g, p: (g, begin + p)),
            pl.BlockSpec((GROUP, PART, HEAD), lambda g, p: (g, p, 0)),
        ],
        out_specs=pl.BlockSpec((HEADS // 2 * TOK, 2 * HEAD), lambda g, p: (0, 0)),
        out_shape=jax.ShapeDtypeStruct((HEADS // 2 * TOK, 2 * HEAD), jnp.float32),
        scratch_shapes=[
            pltpu.VMEM((HEADS // 2 * TOK, GROUP * PART), jnp.bfloat16),
            pltpu.VMEM((GROUP * PART, 2 * HEAD), jnp.bfloat16),
        ],
        compiler_params=pltpu.CompilerParams(vmem_limit_bytes=32 * 1024 * 1024),
        cost_estimate=cost(12 * parts),
        name="mix",
    )(codes, codes, weights, values)


def shards(queries, keys, values, mem_keys, mem_values, knn_index, block_slot, gate_bias, w_out):
    send = functools.partial(
        lax.all_to_all, axis_name=("seq", "mem"), split_axis=0, concat_axis=0, tiled=True
    )
    planes = lax.axis_size("seq")
    near = lax.axis_size("mem")
    near_queries = lax.all_gather(turn(queries[0]), "mem", axis=0, tiled=True).reshape(near, HEADS * TOK, HEAD)
    line_keys = lax.all_gather(mem_keys, "seq", axis=0, tiled=True)
    own = jnp.concatenate([keys[0], values[0]], axis=1)
    blocks = [own] + [
        lax.ppermute(own, "seq", [(i, i + back) for i in range(planes - back)]) for back in range(1, planes)
    ]

    lookups = knn_index[0].transpose(1, 0, 2).reshape(TOK * HEADS * TOPK // ROWS, ROWS)
    asked, places = route(lookups, block_slot)
    wanted = lax.all_to_all(
        asked.reshape(planes, near, CAP + 128), "mem", split_axis=1, concat_axis=1, tiled=True
    )
    codes = lax.all_to_all(wanted, "seq", split_axis=0, concat_axis=0, tiled=True).reshape(DEVS, CAP + 128)
    wanted = wanted.reshape(DEVS, CAP + 128)

    query = queries[0].reshape(TOK, HEADS, HEAD)
    seen = jnp.concatenate(blocks, axis=0)
    key_rows = seen[:, : HEADS * HEAD].reshape(-1, HEADS, HEAD)
    value_rows = seen[:, HEADS * HEAD :].reshape(-1, HEADS, HEAD)
    local = jnp.einsum("qhd,khd->hqk", query, key_rows, preferred_element_type=jnp.float32) * HEAD ** (-0.5)
    back = jnp.arange(seen.shape[0], dtype=jnp.int32) // TOK
    within = jnp.arange(seen.shape[0], dtype=jnp.int32) % TOK
    here = (back == 0)[None, :] & (within[None, :] <= jnp.arange(TOK, dtype=jnp.int32)[:, None])
    earlier = (back > 0) & (back <= lax.axis_index("seq"))
    local = jnp.where((here | earlier[None, :])[None], local, -jnp.inf)
    probs = jax.nn.softmax(local, axis=-1).astype(jnp.bfloat16)
    local_out = jnp.einsum("hqk,khd->hqd", probs, value_rows, preferred_element_type=jnp.float32)
    picked, later = pick(codes, mem_values, local_out)
    first = send(picked)
    scored, later = score(wanted, near_queries, line_keys, later)
    scored = join(scored, first).reshape(planes, near, CAP)
    scores = lax.all_to_all(scored, "mem", split_axis=1, concat_axis=1, tiled=True).reshape(DEVS, CAP)
    last = send(later)
    weights = weigh(places, scores)
    sums = mix(asked, weights, first, 0) + mix(asked, weights, last, PARTS - 1)
    mem_out = jnp.concatenate([sums[:, :HEAD], sums[:, HEAD:]], axis=0).reshape(HEADS, TOK, HEAD)

    gate = jax.nn.sigmoid(gate_bias)[:, None, None]
    combined = (gate * mem_out + (1.0 - gate) * local_out).astype(jnp.bfloat16)
    combined = combined.transpose(1, 0, 2).reshape(TOK, HEADS * HEAD)
    mixed = jnp.dot(combined, w_out, preferred_element_type=jnp.float32).astype(jnp.bfloat16)
    return mixed[None]


def solution(mesh):
    return jax.shard_map(
        shards,
        mesh=mesh,
        in_specs=(
            P("mem", "seq", None),
            P("mem", "seq", None),
            P("mem", "seq", None),
            P(("seq", "mem"), None),
            P(("seq", "mem"), None),
            P("mem", "seq", None, None),
            P(),
            P(),
            P(),
        ),
        out_specs=P("mem", "seq", None),
        check_vma=False,
    )
```

```python
import functools

import jax
import jax.numpy as jnp
from jax import lax
from jax.experimental import pallas as pl
from jax.experimental.pallas import tpu as pltpu
from jax.sharding import PartitionSpec as P

DEVS = 128
TOK = 128
HEADS = 8
HEAD = 128
TOPK = 32
MEM_DEV = 512
BLOCK = 64
CAP = 384
PART = 128
PARTS = CAP // PART
GROUP = 8
PICK = 16
BATCH = 8
ROWS = 256
WINDOW = 80
NT = (((1,), (1,)), ((), ()))


def one_hot(mask):
    return jnp.where(mask, 1.0, 0.0).astype(jnp.bfloat16)


def cost(micros):
    return pl.CostEstimate(flops=int(micros * 1e9), bytes_accessed=int(micros * 1e6), transcendentals=0)


def route_kernel(look_ref, slot_ref, req_ref, place_ref, store, total, slots, parts, starts):
    table = [jnp.broadcast_to(slot_ref[r : r + 1, :], (8, 128)) for r in range(8)]

    def translate(i, carry):
        base = pl.multiple_of(i * 8, 8)
        for half in range(ROWS // 128):
            look = look_ref[pl.ds(base, 8), half * 128 : (half + 1) * 128]
            blk = look >> 6
            low = blk & 127
            high = blk >> 7
            place = jnp.zeros((8, 128), jnp.int32)
            for r in range(8):
                place = jnp.where(high == r, jnp.take_along_axis(table[r], low, axis=1), place)
            store[pl.ds(base, 8), half * 128 : (half + 1) * 128] = place * BLOCK + (look & (BLOCK - 1))
        return carry

    lax.fori_loop(0, look_ref.shape[0] // 8, translate, 0)
    total[...] = jnp.zeros_like(total)
    starts[...] = jnp.zeros_like(starts)
    heads = lax.broadcasted_iota(jnp.int32, starts.shape, 1)
    upper = one_hot(
        lax.broadcasted_iota(jnp.int32, (ROWS, ROWS), 0) <= lax.broadcasted_iota(jnp.int32, (ROWS, ROWS), 1)
    )
    owners = lax.broadcasted_iota(jnp.int32, (DEVS, ROWS), 0)
    ranks = lax.broadcasted_iota(jnp.int32, (CAP, ROWS), 0)
    lane = lax.broadcasted_iota(jnp.int32, (1, ROWS), 1)
    batch = BATCH
    per_head = TOK * TOPK // ROWS

    def place(i, run):
        base = pl.multiple_of(i * batch, batch)
        rows = store[pl.ds(base, batch), :]
        starts[...] = jnp.where((heads * per_head == base) & (heads < HEADS), run[:, :128], starts[...])
        places = []
        for b in range(batch):
            row = base + b
            head = row // per_head
            tok = (row % per_head) * (ROWS // TOPK) + lane // TOPK
            here = rows[b : b + 1, :]
            owner = here // MEM_DEV
            mine = jnp.where(owners == owner, 1.0, 0.0)
            count = jnp.dot(mine.astype(jnp.bfloat16), upper, preferred_element_type=jnp.float32) + run
            rank = jnp.sum(mine * count, axis=0, keepdims=True).astype(jnp.int32) - 1
            run = jnp.broadcast_to(count[:, ROWS - 1 :], (DEVS, ROWS))
            places.append(owner * MEM_DEV + rank)
            span = slice(b * ROWS, (b + 1) * ROWS)
            slots[:, span] = one_hot(ranks == rank)
            local = here & (MEM_DEV - 1)
            first = (local & 255).astype(jnp.float32)
            second = ((local >> 8) + 2 * tok).astype(jnp.float32)
            parts[0:DEVS, span] = (mine * first).astype(jnp.bfloat16)
            parts[DEVS : 2 * DEVS, span] = (mine * second).astype(jnp.bfloat16)
            parts[2 * DEVS :, span] = (mine * (head + 1).astype(jnp.float32)).astype(jnp.bfloat16)
        total[...] += lax.dot_general(parts[...], slots[...], NT, preferred_element_type=jnp.float32)
        place_ref[pl.ds(base, batch), :] = jnp.concatenate(places, axis=0)
        return run

    run = lax.fori_loop(0, look_ref.shape[0] // batch, place, jnp.zeros((DEVS, ROWS), jnp.float32))
    first = total[0:DEVS, :].astype(jnp.int32)
    second = total[DEVS : 2 * DEVS, :].astype(jnp.int32)
    third = total[2 * DEVS :, :].astype(jnp.int32)
    local = first + (second & 1) * 256
    query = (third - 1) * TOK + (second >> 1)
    req_ref[:, :CAP] = jnp.where(third > 0, query * MEM_DEV + local, -1)
    req_ref[:, CAP:] = jnp.where(heads == HEADS, run[:, :128], starts[...]).astype(jnp.int32)


def route(lookups, block_slot):
    return pl.pallas_call(
        route_kernel,
        out_shape=[
            jax.ShapeDtypeStruct((DEVS, CAP + 128), jnp.int32),
            jax.ShapeDtypeStruct((TOK * HEADS * TOPK // ROWS, ROWS), jnp.int32),
        ],
        scratch_shapes=[
            pltpu.VMEM((TOK * HEADS * TOPK // ROWS, ROWS), jnp.int32),
            pltpu.VMEM((3 * DEVS, CAP), jnp.float32),
            pltpu.VMEM((CAP, BATCH * ROWS), jnp.bfloat16),
            pltpu.VMEM((3 * DEVS, BATCH * ROWS), jnp.bfloat16),
            pltpu.VMEM((DEVS, 128), jnp.float32),
        ],
        compiler_params=pltpu.CompilerParams(vmem_limit_bytes=32 * 1024 * 1024),
        cost_estimate=cost(22),
        name="route",
    )(lookups, block_slot.reshape(8, 128))


def turn_kernel(query_ref, out_ref):
    for h in range(HEADS):
        out_ref[h * TOK : (h + 1) * TOK, :] = query_ref[:, h * HEAD : (h + 1) * HEAD]


def turn(queries):
    return pl.pallas_call(
        turn_kernel,
        out_shape=jax.ShapeDtypeStruct((HEADS * TOK, HEAD), jnp.bfloat16),
        name="turn",
    )(queries)


def pick_rows(code_ref, start_ref, mem_ref, wanted, found, hot):
    group = code_ref.shape[0]

    @pl.when(pl.program_id(0) == 0)
    def _():
        wanted[CAP:, :] = jnp.full((WINDOW, group), -1.0, jnp.float32)
        found[...] = jnp.zeros_like(found)

    for part in range(PARTS):
        span = slice(part * PART, (part + 1) * PART)
        code = jnp.transpose(code_ref[:, span])
        wanted[span, :] = ((code & (MEM_DEV - 1)) + (code >> 16) * MEM_DEV).astype(jnp.float32)
    lanes = lax.broadcasted_iota(jnp.int32, (WINDOW, 128), 1).astype(jnp.float32)
    lane_ids = [lanes.astype(jnp.bfloat16), (lanes + 128).astype(jnp.bfloat16)]

    def product(h, spots, hot):
        for i, at in enumerate(spots):
            col = jnp.broadcast_to(wanted[pl.ds(at, WINDOW), i : i + 1], (WINDOW, 128))
            low = (col - h * MEM_DEV).astype(jnp.bfloat16)
            high = (col - (h * MEM_DEV + 256)).astype(jnp.bfloat16)
            for k, part in enumerate((low, low, high, high)):
                hot[i * WINDOW : (i + 1) * WINDOW, k * 128 : (k + 1) * 128] = jnp.where(
                    part == lane_ids[k % 2], jnp.bfloat16(1), jnp.bfloat16(0)
                )
        return jnp.dot(hot[...], mem_ref[:, h * HEAD : (h + 1) * HEAD], preferred_element_type=jnp.float32)

    def keep(h, i, at, rows):
        head = wanted[pl.ds(at, rows.shape[0]), i : i + 1]
        own = (head >= h * MEM_DEV) & (head < (h + 1) * MEM_DEV)
        found[i, pl.ds(at, rows.shape[0]), :] = jnp.where(own, rows, found[i, pl.ds(at, rows.shape[0]), :])

    begins = [[start_ref[i, h] // 8 * 8 for i in range(group)] for h in range(HEADS)]
    for h in range(HEADS):
        spots = [pl.multiple_of(at, 8) for at in begins[h]]
        rows = product(h, spots, hot.at[h % 2])
        for i, at in enumerate(spots):
            mine = rows[i * WINDOW : (i + 1) * WINDOW]
            keep(h, i, at, mine[:8])
            found[i, pl.ds(at + 8, WINDOW - 8), :] = mine[8:]

    for h in range(HEADS):
        most = start_ref[0, h + 1] - begins[h][0]
        for i in range(1, group):
            most = jnp.maximum(most, start_ref[i, h + 1] - begins[h][i])

        def one_window(w, carry, h=h):
            spots = [pl.multiple_of(jnp.minimum(at + w * WINDOW, CAP), 8) for at in begins[h]]
            rows = product(h, spots, hot.at[0])
            for i, at in enumerate(spots):
                keep(h, i, at, rows[i * WINDOW : (i + 1) * WINDOW])
            return carry

        lax.fori_loop(1, (most + WINDOW - 1) // WINDOW, one_window, 0)


def pick_specs(group):
    specs = [
        pl.BlockSpec((group, CAP), lambda g: (g, 0)),
        pl.BlockSpec((group, 128), lambda g: (g, CAP // 128), memory_space=pltpu.SMEM),
    ]
    scratch = [
        pltpu.VMEM((CAP + WINDOW, group), jnp.float32),
        pltpu.VMEM((group, CAP + WINDOW, HEAD), jnp.float32),
        pltpu.VMEM((2, group * WINDOW, MEM_DEV), jnp.bfloat16),
    ]
    return specs, scratch


def pick_kernel(code_ref, start_ref, value_ref, _, first_ref, last_ref, wanted, found, hot):
    pick_rows(code_ref, start_ref, value_ref, wanted, found, hot)
    for i in range(code_ref.shape[0]):
        first_ref[i] = found[i, : CAP - PART, :].astype(jnp.bfloat16)
        last_ref[i] = found[i, CAP - PART : CAP, :].astype(jnp.bfloat16)


def pick(codes, values, ready):
    specs, scratch = pick_specs(PICK)
    sizes = (CAP - PART, PART)
    return pl.pallas_call(
        pick_kernel,
        grid=(DEVS // PICK,),
        in_specs=specs
        + [pl.BlockSpec((MEM_DEV, HEADS * HEAD), lambda g: (0, 0)), pl.BlockSpec(memory_space=pl.ANY)],
        out_specs=[pl.BlockSpec((PICK, size, HEAD), lambda g: (g, 0, 0)) for size in sizes],
        out_shape=[pltpu.HBM((DEVS, size, HEAD), jnp.bfloat16) for size in sizes],
        scratch_shapes=scratch,
        compiler_params=pltpu.CompilerParams(vmem_limit_bytes=40 * 1024 * 1024),
        cost_estimate=cost(40),
        name="pick",
    )(codes, codes, values, ready)


def score_kernel(code_ref, start_ref, key_ref, query_ref, _, out_ref, __, wanted, found, hot):
    pick_rows(code_ref, start_ref, key_ref, wanted, found, hot)
    ids = lax.broadcasted_iota(jnp.int32, (HEADS * TOK, CAP), 0)
    for i in range(GROUP):
        keys = found[i, :CAP, :].astype(jnp.bfloat16)
        every = lax.dot_general(query_ref[i], keys, NT, preferred_element_type=jnp.float32)
        own = ids == code_ref[i : i + 1, :] >> 9
        out_ref[i : i + 1, :] = jnp.sum(jnp.where(own, every, 0.0), axis=0, keepdims=True) * HEAD ** (-0.5)


def score(codes, queries, keys, through):
    near = queries.shape[0] // GROUP
    specs, scratch = pick_specs(GROUP)
    return pl.pallas_call(
        score_kernel,
        grid=(DEVS // GROUP,),
        in_specs=specs
        + [
            pl.BlockSpec((MEM_DEV, HEADS * HEAD), lambda g: (g // near, 0)),
            pl.BlockSpec((GROUP, HEADS * TOK, HEAD), lambda g: (g % near, 0, 0)),
            pl.BlockSpec(memory_space=pl.ANY),
        ],
        out_specs=[specs[0], pl.BlockSpec(memory_space=pl.ANY)],
        out_shape=[
            jax.ShapeDtypeStruct((DEVS, CAP), jnp.float32),
            jax.ShapeDtypeStruct(through.shape, through.dtype),
        ],
        scratch_shapes=scratch,
        input_output_aliases={4: 1},
        compiler_params=pltpu.CompilerParams(vmem_limit_bytes=40 * 1024 * 1024),
        cost_estimate=cost(75),
        name="score",
    )(codes, codes, keys, queries, through)


def join_kernel(a_ref, _, __, out_ref):
    out_ref[...] = a_ref[...]


def join(scores, *ready):
    return pl.pallas_call(
        join_kernel,
        in_specs=[pl.BlockSpec(memory_space=pltpu.VMEM)] + [pl.BlockSpec(memory_space=pl.ANY)] * len(ready),
        out_shape=jax.ShapeDtypeStruct(scores.shape, scores.dtype),
        name="join",
    )(scores, *ready)


def weigh_kernel(place_ref, score_ref, out_ref, parts, near, total, slots, spread):
    score = score_ref[...]
    for part in range(3):
        piece = score.astype(jnp.bfloat16)
        parts[part * DEVS : (part + 1) * DEVS, :] = piece
        score = score - piece.astype(jnp.float32)
    owners = lax.broadcasted_iota(jnp.int32, (DEVS, ROWS), 0)
    ranks = lax.broadcasted_iota(jnp.int32, (CAP, ROWS), 0)
    batches = place_ref.shape[0] // BATCH

    def fetch(i, carry):
        base = pl.multiple_of(i * BATCH, BATCH)
        place = place_ref[pl.ds(base, BATCH), :]
        rows = []
        for b in range(BATCH):
            here = place[b : b + 1, :]
            hot = one_hot(ranks == (here & (MEM_DEV - 1)))
            each = jnp.dot(parts[...], hot, preferred_element_type=jnp.float32)
            each = (each[:DEVS] + each[DEVS : 2 * DEVS]) + each[2 * DEVS :]
            rows.append(jnp.sum(jnp.where(owners == here // MEM_DEV, each, 0.0), axis=0, keepdims=True))
        near[pl.ds(base, BATCH), :] = jnp.concatenate(rows, axis=0)
        return carry

    lax.fori_loop(0, batches, fetch, 0)
    lane = lax.broadcasted_iota(jnp.int32, near.shape, 1)

    def across(x, op):
        for k in (16, 8, 4, 2, 1):
            other = jnp.where((lane & k) > 0, pltpu.roll(x, k, 1), pltpu.roll(x, ROWS - k, 1))
            x = op(x, other)
        return x

    score = near[...]
    power = jnp.exp(score - across(score, jnp.maximum))
    near[...] = power / across(power, jnp.add)
    total[...] = jnp.zeros_like(total)

    def scatter(i, carry):
        base = pl.multiple_of(i * BATCH, BATCH)
        place = place_ref[pl.ds(base, BATCH), :]
        prob = near[pl.ds(base, BATCH), :]
        for b in range(BATCH):
            here = place[b : b + 1, :]
            span = slice(b * ROWS, (b + 1) * ROWS)
            slots[:, span] = one_hot(ranks == (here & (MEM_DEV - 1)))
            mine = owners == here // MEM_DEV
            spread[:, span] = jnp.where(mine, prob[b : b + 1, :], 0.0).astype(jnp.bfloat16)
        total[...] += lax.dot_general(spread[...], slots[...], NT, preferred_element_type=jnp.float32)
        return carry

    lax.fori_loop(0, batches, scatter, 0)
    out_ref[...] = total[...]


def weigh(places, scores):
    return pl.pallas_call(
        weigh_kernel,
        out_shape=jax.ShapeDtypeStruct((DEVS, CAP), jnp.float32),
        scratch_shapes=[
            pltpu.VMEM((3 * DEVS, CAP), jnp.bfloat16),
            pltpu.VMEM(places.shape, jnp.float32),
            pltpu.VMEM((DEVS, CAP), jnp.float32),
            pltpu.VMEM((CAP, BATCH * ROWS), jnp.bfloat16),
            pltpu.VMEM((DEVS, BATCH * ROWS), jnp.bfloat16),
        ],
        compiler_params=pltpu.CompilerParams(vmem_limit_bytes=32 * 1024 * 1024),
        cost_estimate=cost(22),
        name="weigh",
    )(places, scores)


def mix_kernel(code_ref, start_ref, weight_ref, value_ref, out_ref, spread, rows, *, begin):
    part = pl.program_id(1)
    half = HEADS // 2

    @pl.when((pl.program_id(0) == 0) & (part == 0))
    def _():
        out_ref[...] = jnp.zeros_like(out_ref)

    slot = lax.broadcasted_iota(jnp.int32, (PART, HEAD), 0).astype(jnp.float32).astype(jnp.bfloat16)
    for i in range(GROUP):
        span = slice(i * PART, (i + 1) * PART)
        first = jnp.clip(start_ref[i, half] - (begin + part) * PART, 0, PART)
        later = slot >= first.astype(jnp.float32).astype(jnp.bfloat16)
        value = value_ref[i]
        rows[span, :HEAD] = jnp.where(later, jnp.bfloat16(0), value)
        rows[span, HEAD:] = jnp.where(later, value, jnp.bfloat16(0))
        query = (code_ref[i : i + 1, :] >> 9) & (half * TOK - 1)
        weight = weight_ref[i : i + 1, :]
        for h in range(half):
            ids = lax.broadcasted_iota(jnp.int32, (TOK, PART), 0) + h * TOK
            spread[h * TOK : (h + 1) * TOK, span] = jnp.where(ids == query, weight, 0.0).astype(jnp.bfloat16)
    out_ref[...] += jnp.dot(spread[...], rows[...], preferred_element_type=jnp.float32)


def mix(codes, weights, values, begin):
    parts = values.shape[1] // PART
    return pl.pallas_call(
        functools.partial(mix_kernel, begin=begin),
        grid=(DEVS // GROUP, parts),
        in_specs=[
            pl.BlockSpec((GROUP, PART), lambda g, p: (g, begin + p)),
            pl.BlockSpec((GROUP, 128), lambda g, p: (g, CAP // 128), memory_space=pltpu.SMEM),
            pl.BlockSpec((GROUP, PART), lambda g, p: (g, begin + p)),
            pl.BlockSpec((GROUP, PART, HEAD), lambda g, p: (g, p, 0)),
        ],
        out_specs=pl.BlockSpec((HEADS // 2 * TOK, 2 * HEAD), lambda g, p: (0, 0)),
        out_shape=jax.ShapeDtypeStruct((HEADS // 2 * TOK, 2 * HEAD), jnp.float32),
        scratch_shapes=[
            pltpu.VMEM((HEADS // 2 * TOK, GROUP * PART), jnp.bfloat16),
            pltpu.VMEM((GROUP * PART, 2 * HEAD), jnp.bfloat16),
        ],
        compiler_params=pltpu.CompilerParams(vmem_limit_bytes=32 * 1024 * 1024),
        cost_estimate=cost(12 * parts),
        name="mix",
    )(codes, codes, weights, values)


def shards(queries, keys, values, mem_keys, mem_values, knn_index, block_slot, gate_bias, w_out):
    send = functools.partial(
        lax.all_to_all, axis_name=("seq", "mem"), split_axis=0, concat_axis=0, tiled=True
    )
    planes = lax.axis_size("seq")
    near = lax.axis_size("mem")
    near_queries = lax.all_gather(turn(queries[0]), "mem", axis=0, tiled=True).reshape(near, HEADS * TOK, HEAD)
    up = [(i, (i + 1) % planes) for i in range(planes)]
    down = [(i, (i - 1) % planes) for i in range(planes)]
    middle = mem_keys.shape[0] // 2
    below = lax.ppermute(mem_keys, "seq", up)
    above = lax.ppermute(mem_keys, "seq", down)
    far = jnp.concatenate(
        [lax.ppermute(below[:middle], "seq", up), lax.ppermute(above[middle:], "seq", down)], axis=0
    )
    place = lax.axis_index("seq")
    line_keys = jnp.zeros((planes * MEM_DEV, HEADS * HEAD), mem_keys.dtype)
    for back, rows in enumerate((mem_keys, below, far, above)):
        line_keys = lax.dynamic_update_slice_in_dim(line_keys, rows, (place - back) % planes * MEM_DEV, axis=0)
    own = jnp.concatenate([keys[0], values[0]], axis=1)
    blocks = [own] + [
        lax.ppermute(own, "seq", [(i, i + back) for i in range(planes - back)]) for back in range(1, planes)
    ]

    lookups = knn_index[0].transpose(1, 0, 2).reshape(TOK * HEADS * TOPK // ROWS, ROWS)
    asked, places = route(lookups, block_slot)
    wanted = lax.all_to_all(
        asked.reshape(planes, near, CAP + 128), "mem", split_axis=1, concat_axis=1, tiled=True
    )
    codes = lax.all_to_all(wanted, "seq", split_axis=0, concat_axis=0, tiled=True).reshape(DEVS, CAP + 128)
    wanted = wanted.reshape(DEVS, CAP + 128)

    query = queries[0].reshape(TOK, HEADS, HEAD)
    seen = jnp.concatenate(blocks, axis=0)
    key_rows = seen[:, : HEADS * HEAD].reshape(-1, HEADS, HEAD)
    value_rows = seen[:, HEADS * HEAD :].reshape(-1, HEADS, HEAD)
    local = jnp.einsum("qhd,khd->hqk", query, key_rows, preferred_element_type=jnp.float32) * HEAD ** (-0.5)
    back = jnp.arange(seen.shape[0], dtype=jnp.int32) // TOK
    within = jnp.arange(seen.shape[0], dtype=jnp.int32) % TOK
    here = (back == 0)[None, :] & (within[None, :] <= jnp.arange(TOK, dtype=jnp.int32)[:, None])
    earlier = (back > 0) & (back <= lax.axis_index("seq"))
    local = jnp.where((here | earlier[None, :])[None], local, -jnp.inf)
    probs = jax.nn.softmax(local, axis=-1).astype(jnp.bfloat16)
    local_out = jnp.einsum("hqk,khd->hqd", probs, value_rows, preferred_element_type=jnp.float32)
    picked, later = pick(codes, mem_values, line_keys)
    first = send(picked)
    scored, later = score(wanted, near_queries, line_keys, later)
    scored = join(scored, first, local_out).reshape(planes, near, CAP)
    scores = lax.all_to_all(scored, "mem", split_axis=1, concat_axis=1, tiled=True).reshape(DEVS, CAP)
    last = send(later)
    weights = weigh(places, scores)
    sums = mix(asked, weights, first, 0) + mix(asked, weights, last, PARTS - 1)
    mem_out = jnp.concatenate([sums[:, :HEAD], sums[:, HEAD:]], axis=0).reshape(HEADS, TOK, HEAD)

    gate = jax.nn.sigmoid(gate_bias)[:, None, None]
    combined = (gate * mem_out + (1.0 - gate) * local_out).astype(jnp.bfloat16)
    combined = combined.transpose(1, 0, 2).reshape(TOK, HEADS * HEAD)
    mixed = jnp.dot(combined, w_out, preferred_element_type=jnp.float32).astype(jnp.bfloat16)
    return mixed[None]


def solution(mesh):
    return jax.shard_map(
        shards,
        mesh=mesh,
        in_specs=(
            P("mem", "seq", None),
            P("mem", "seq", None),
            P("mem", "seq", None),
            P(("seq", "mem"), None),
            P(("seq", "mem"), None),
            P("mem", "seq", None, None),
            P(),
            P(),
            P(),
        ),
        out_specs=P("mem", "seq", None),
        check_vma=False,
    )
```

```python
import functools

import jax
import jax.numpy as jnp
from jax import lax
from jax.experimental import pallas as pl
from jax.experimental.pallas import tpu as pltpu
from jax.sharding import PartitionSpec as P

DEVS = 128
TOK = 128
HEADS = 8
HEAD = 128
TOPK = 32
MEM_DEV = 512
BLOCK = 64
CAP = 384
PART = 128
PARTS = CAP // PART
GROUP = 8
PICK = 16
BATCH = 8
ROWS = 256
WINDOW = 80
NT = (((1,), (1,)), ((), ()))


def one_hot(mask):
    return jnp.where(mask, 1.0, 0.0).astype(jnp.bfloat16)


def cost(micros):
    return pl.CostEstimate(flops=int(micros * 1e9), bytes_accessed=int(micros * 1e6), transcendentals=0)


def route_kernel(look_ref, slot_ref, req_ref, place_ref, store, total, slots, parts, starts):
    table = [jnp.broadcast_to(slot_ref[r : r + 1, :], (8, 128)) for r in range(8)]

    def translate(i, carry):
        base = pl.multiple_of(i * 8, 8)
        for half in range(ROWS // 128):
            look = look_ref[pl.ds(base, 8), half * 128 : (half + 1) * 128]
            blk = look >> 6
            low = blk & 127
            high = blk >> 7
            place = jnp.zeros((8, 128), jnp.int32)
            for r in range(8):
                place = jnp.where(high == r, jnp.take_along_axis(table[r], low, axis=1), place)
            store[pl.ds(base, 8), half * 128 : (half + 1) * 128] = place * BLOCK + (look & (BLOCK - 1))
        return carry

    lax.fori_loop(0, look_ref.shape[0] // 8, translate, 0)
    total[...] = jnp.zeros_like(total)
    starts[...] = jnp.zeros_like(starts)
    heads = lax.broadcasted_iota(jnp.int32, starts.shape, 1)
    upper = one_hot(
        lax.broadcasted_iota(jnp.int32, (ROWS, ROWS), 0) <= lax.broadcasted_iota(jnp.int32, (ROWS, ROWS), 1)
    )
    owners = lax.broadcasted_iota(jnp.int32, (DEVS, ROWS), 0)
    ranks = lax.broadcasted_iota(jnp.int32, (CAP, ROWS), 0)
    lane = lax.broadcasted_iota(jnp.int32, (1, ROWS), 1)
    batch = BATCH
    per_head = TOK * TOPK // ROWS

    def place(i, run):
        base = pl.multiple_of(i * batch, batch)
        rows = store[pl.ds(base, batch), :]
        starts[...] = jnp.where((heads * per_head == base) & (heads < HEADS), run[:, :128], starts[...])
        places = []
        for b in range(batch):
            row = base + b
            head = row // per_head
            tok = (row % per_head) * (ROWS // TOPK) + lane // TOPK
            here = rows[b : b + 1, :]
            owner = here // MEM_DEV
            mine = jnp.where(owners == owner, 1.0, 0.0)
            count = jnp.dot(mine.astype(jnp.bfloat16), upper, preferred_element_type=jnp.float32) + run
            rank = jnp.sum(mine * count, axis=0, keepdims=True).astype(jnp.int32) - 1
            run = jnp.broadcast_to(count[:, ROWS - 1 :], (DEVS, ROWS))
            places.append(owner * MEM_DEV + rank)
            span = slice(b * ROWS, (b + 1) * ROWS)
            slots[:, span] = one_hot(ranks == rank)
            local = here & (MEM_DEV - 1)
            first = (local & 255).astype(jnp.float32)
            second = ((local >> 8) + 2 * tok).astype(jnp.float32)
            parts[0:DEVS, span] = (mine * first).astype(jnp.bfloat16)
            parts[DEVS : 2 * DEVS, span] = (mine * second).astype(jnp.bfloat16)
            parts[2 * DEVS :, span] = (mine * (head + 1).astype(jnp.float32)).astype(jnp.bfloat16)
        total[...] += lax.dot_general(parts[...], slots[...], NT, preferred_element_type=jnp.float32)
        place_ref[pl.ds(base, batch), :] = jnp.concatenate(places, axis=0)
        return run

    run = lax.fori_loop(0, look_ref.shape[0] // batch, place, jnp.zeros((DEVS, ROWS), jnp.float32))
    first = total[0:DEVS, :].astype(jnp.int32)
    second = total[DEVS : 2 * DEVS, :].astype(jnp.int32)
    third = total[2 * DEVS :, :].astype(jnp.int32)
    local = first + (second & 1) * 256
    query = (third - 1) * TOK + (second >> 1)
    req_ref[:, :CAP] = jnp.where(third > 0, query * MEM_DEV + local, -1)
    req_ref[:, CAP:] = jnp.where(heads == HEADS, run[:, :128], starts[...]).astype(jnp.int32)


def route(lookups, block_slot):
    return pl.pallas_call(
        route_kernel,
        out_shape=[
            jax.ShapeDtypeStruct((DEVS, CAP + 128), jnp.int32),
            jax.ShapeDtypeStruct((TOK * HEADS * TOPK // ROWS, ROWS), jnp.int32),
        ],
        scratch_shapes=[
            pltpu.VMEM((TOK * HEADS * TOPK // ROWS, ROWS), jnp.int32),
            pltpu.VMEM((3 * DEVS, CAP), jnp.float32),
            pltpu.VMEM((CAP, BATCH * ROWS), jnp.bfloat16),
            pltpu.VMEM((3 * DEVS, BATCH * ROWS), jnp.bfloat16),
            pltpu.VMEM((DEVS, 128), jnp.float32),
        ],
        compiler_params=pltpu.CompilerParams(vmem_limit_bytes=32 * 1024 * 1024),
        cost_estimate=cost(22),
        name="route",
    )(lookups, block_slot.reshape(8, 128))


def turn_kernel(query_ref, out_ref):
    for h in range(HEADS):
        out_ref[h * TOK : (h + 1) * TOK, :] = query_ref[:, h * HEAD : (h + 1) * HEAD]


def turn(queries):
    return pl.pallas_call(
        turn_kernel,
        out_shape=jax.ShapeDtypeStruct((HEADS * TOK, HEAD), jnp.bfloat16),
        name="turn",
    )(queries)


def pick_rows(code_ref, start_ref, mem_ref, wanted, found, hot):
    group = code_ref.shape[0]

    @pl.when(pl.program_id(0) == 0)
    def _():
        wanted[CAP:, :] = jnp.full((WINDOW, group), -1.0, jnp.float32)
        found[...] = jnp.zeros_like(found)

    for part in range(PARTS):
        span = slice(part * PART, (part + 1) * PART)
        code = jnp.transpose(code_ref[:, span])
        wanted[span, :] = ((code & (MEM_DEV - 1)) + (code >> 16) * MEM_DEV).astype(jnp.float32)
    lanes = lax.broadcasted_iota(jnp.int32, (WINDOW, 128), 1).astype(jnp.float32)
    lane_ids = [lanes.astype(jnp.bfloat16), (lanes + 128).astype(jnp.bfloat16)]

    def product(h, spots, hot):
        for i, at in enumerate(spots):
            col = jnp.broadcast_to(wanted[pl.ds(at, WINDOW), i : i + 1], (WINDOW, 128))
            low = (col - h * MEM_DEV).astype(jnp.bfloat16)
            high = (col - (h * MEM_DEV + 256)).astype(jnp.bfloat16)
            for k, part in enumerate((low, low, high, high)):
                hot[i * WINDOW : (i + 1) * WINDOW, k * 128 : (k + 1) * 128] = jnp.where(
                    part == lane_ids[k % 2], jnp.bfloat16(1), jnp.bfloat16(0)
                )
        return jnp.dot(hot[...], mem_ref[:, h * HEAD : (h + 1) * HEAD], preferred_element_type=jnp.float32)

    def keep(h, i, at, rows):
        head = wanted[pl.ds(at, rows.shape[0]), i : i + 1]
        own = (head >= h * MEM_DEV) & (head < (h + 1) * MEM_DEV)
        found[i, pl.ds(at, rows.shape[0]), :] = jnp.where(own, rows, found[i, pl.ds(at, rows.shape[0]), :])

    begins = [[start_ref[i, h] // 8 * 8 for i in range(group)] for h in range(HEADS)]
    for h in range(HEADS):
        spots = [pl.multiple_of(at, 8) for at in begins[h]]
        rows = product(h, spots, hot.at[h % 2])
        for i, at in enumerate(spots):
            mine = rows[i * WINDOW : (i + 1) * WINDOW]
            keep(h, i, at, mine[:8])
            found[i, pl.ds(at + 8, WINDOW - 8), :] = mine[8:]

    for h in range(HEADS):
        most = start_ref[0, h + 1] - begins[h][0]
        for i in range(1, group):
            most = jnp.maximum(most, start_ref[i, h + 1] - begins[h][i])

        def one_window(w, carry, h=h):
            spots = [pl.multiple_of(jnp.minimum(at + w * WINDOW, CAP), 8) for at in begins[h]]
            rows = product(h, spots, hot.at[0])
            for i, at in enumerate(spots):
                keep(h, i, at, rows[i * WINDOW : (i + 1) * WINDOW])
            return carry

        lax.fori_loop(1, (most + WINDOW - 1) // WINDOW, one_window, 0)


def pick_specs(group):
    specs = [
        pl.BlockSpec((group, CAP), lambda g: (g, 0)),
        pl.BlockSpec((group, 128), lambda g: (g, CAP // 128), memory_space=pltpu.SMEM),
    ]
    scratch = [
        pltpu.VMEM((CAP + WINDOW, group), jnp.float32),
        pltpu.VMEM((group, CAP + WINDOW, HEAD), jnp.float32),
        pltpu.VMEM((2, group * WINDOW, MEM_DEV), jnp.bfloat16),
    ]
    return specs, scratch


def pick_kernel(code_ref, start_ref, value_ref, _, first_ref, last_ref, wanted, found, hot):
    pick_rows(code_ref, start_ref, value_ref, wanted, found, hot)
    for i in range(code_ref.shape[0]):
        first_ref[i] = found[i, : CAP - PART, :].astype(jnp.bfloat16)
        last_ref[i] = found[i, CAP - PART : CAP, :].astype(jnp.bfloat16)


def pick(codes, values, ready):
    specs, scratch = pick_specs(PICK)
    sizes = (CAP - PART, PART)
    return pl.pallas_call(
        pick_kernel,
        grid=(DEVS // PICK,),
        in_specs=specs
        + [pl.BlockSpec((MEM_DEV, HEADS * HEAD), lambda g: (0, 0)), pl.BlockSpec(memory_space=pl.ANY)],
        out_specs=[pl.BlockSpec((PICK, size, HEAD), lambda g: (g, 0, 0)) for size in sizes],
        out_shape=[pltpu.HBM((DEVS, size, HEAD), jnp.bfloat16) for size in sizes],
        scratch_shapes=scratch,
        compiler_params=pltpu.CompilerParams(vmem_limit_bytes=40 * 1024 * 1024),
        cost_estimate=cost(40),
        name="pick",
    )(codes, codes, values, ready)


def score_kernel(code_ref, start_ref, key_ref, query_ref, _, out_ref, __, wanted, found, hot):
    pick_rows(code_ref, start_ref, key_ref, wanted, found, hot)
    ids = lax.broadcasted_iota(jnp.int32, (HEADS * TOK, CAP), 0)
    for i in range(GROUP):
        keys = found[i, :CAP, :].astype(jnp.bfloat16)
        every = lax.dot_general(query_ref[i], keys, NT, preferred_element_type=jnp.float32)
        own = ids == code_ref[i : i + 1, :] >> 9
        out_ref[i : i + 1, :] = jnp.sum(jnp.where(own, every, 0.0), axis=0, keepdims=True) * HEAD ** (-0.5)


def score(codes, queries, keys, through):
    near = queries.shape[0] // GROUP
    specs, scratch = pick_specs(GROUP)
    return pl.pallas_call(
        score_kernel,
        grid=(DEVS // GROUP,),
        in_specs=specs
        + [
            pl.BlockSpec((MEM_DEV, HEADS * HEAD), lambda g: (g // near, 0)),
            pl.BlockSpec((GROUP, HEADS * TOK, HEAD), lambda g: (g % near, 0, 0)),
            pl.BlockSpec(memory_space=pl.ANY),
        ],
        out_specs=[specs[0], pl.BlockSpec(memory_space=pl.ANY)],
        out_shape=[
            jax.ShapeDtypeStruct((DEVS, CAP), jnp.float32),
            jax.ShapeDtypeStruct(through.shape, through.dtype),
        ],
        scratch_shapes=scratch,
        input_output_aliases={4: 1},
        compiler_params=pltpu.CompilerParams(vmem_limit_bytes=40 * 1024 * 1024),
        cost_estimate=cost(75),
        name="score",
    )(codes, codes, keys, queries, through)


def after_kernel(*refs):
    pass


def after(ready, *arrays):
    count = len(arrays)
    return pl.pallas_call(
        after_kernel,
        in_specs=[pl.BlockSpec(memory_space=pl.ANY)] * (count + 1),
        out_specs=[pl.BlockSpec(memory_space=pl.ANY)] * count,
        out_shape=[jax.ShapeDtypeStruct(one.shape, one.dtype) for one in arrays],
        input_output_aliases={i + 1: i for i in range(count)},
        name="after",
    )(ready, *arrays)


def join_kernel(a_ref, _, __, out_ref):
    out_ref[...] = a_ref[...]


def join(scores, *ready):
    return pl.pallas_call(
        join_kernel,
        in_specs=[pl.BlockSpec(memory_space=pltpu.VMEM)] + [pl.BlockSpec(memory_space=pl.ANY)] * len(ready),
        out_shape=jax.ShapeDtypeStruct(scores.shape, scores.dtype),
        name="join",
    )(scores, *ready)


def weigh_kernel(place_ref, score_ref, out_ref, parts, near, total, slots, spread):
    score = score_ref[...]
    for part in range(3):
        piece = score.astype(jnp.bfloat16)
        parts[part * DEVS : (part + 1) * DEVS, :] = piece
        score = score - piece.astype(jnp.float32)
    owners = lax.broadcasted_iota(jnp.int32, (DEVS, ROWS), 0)
    ranks = lax.broadcasted_iota(jnp.int32, (CAP, ROWS), 0)
    batches = place_ref.shape[0] // BATCH

    def fetch(i, carry):
        base = pl.multiple_of(i * BATCH, BATCH)
        place = place_ref[pl.ds(base, BATCH), :]
        rows = []
        for b in range(BATCH):
            here = place[b : b + 1, :]
            hot = one_hot(ranks == (here & (MEM_DEV - 1)))
            each = jnp.dot(parts[...], hot, preferred_element_type=jnp.float32)
            each = (each[:DEVS] + each[DEVS : 2 * DEVS]) + each[2 * DEVS :]
            rows.append(jnp.sum(jnp.where(owners == here // MEM_DEV, each, 0.0), axis=0, keepdims=True))
        near[pl.ds(base, BATCH), :] = jnp.concatenate(rows, axis=0)
        return carry

    lax.fori_loop(0, batches, fetch, 0)
    lane = lax.broadcasted_iota(jnp.int32, near.shape, 1)

    def across(x, op):
        for k in (16, 8, 4, 2, 1):
            other = jnp.where((lane & k) > 0, pltpu.roll(x, k, 1), pltpu.roll(x, ROWS - k, 1))
            x = op(x, other)
        return x

    score = near[...]
    power = jnp.exp(score - across(score, jnp.maximum))
    near[...] = power / across(power, jnp.add)
    total[...] = jnp.zeros_like(total)

    def scatter(i, carry):
        base = pl.multiple_of(i * BATCH, BATCH)
        place = place_ref[pl.ds(base, BATCH), :]
        prob = near[pl.ds(base, BATCH), :]
        for b in range(BATCH):
            here = place[b : b + 1, :]
            span = slice(b * ROWS, (b + 1) * ROWS)
            slots[:, span] = one_hot(ranks == (here & (MEM_DEV - 1)))
            mine = owners == here // MEM_DEV
            spread[:, span] = jnp.where(mine, prob[b : b + 1, :], 0.0).astype(jnp.bfloat16)
        total[...] += lax.dot_general(spread[...], slots[...], NT, preferred_element_type=jnp.float32)
        return carry

    lax.fori_loop(0, batches, scatter, 0)
    out_ref[...] = total[...]


def weigh(places, scores):
    return pl.pallas_call(
        weigh_kernel,
        out_shape=jax.ShapeDtypeStruct((DEVS, CAP), jnp.float32),
        scratch_shapes=[
            pltpu.VMEM((3 * DEVS, CAP), jnp.bfloat16),
            pltpu.VMEM(places.shape, jnp.float32),
            pltpu.VMEM((DEVS, CAP), jnp.float32),
            pltpu.VMEM((CAP, BATCH * ROWS), jnp.bfloat16),
            pltpu.VMEM((DEVS, BATCH * ROWS), jnp.bfloat16),
        ],
        compiler_params=pltpu.CompilerParams(vmem_limit_bytes=32 * 1024 * 1024),
        cost_estimate=cost(22),
        name="weigh",
    )(places, scores)


def mix_kernel(code_ref, start_ref, weight_ref, value_ref, out_ref, spread, rows, *, begin):
    part = pl.program_id(1)
    half = HEADS // 2

    @pl.when((pl.program_id(0) == 0) & (part == 0))
    def _():
        out_ref[...] = jnp.zeros_like(out_ref)

    slot = lax.broadcasted_iota(jnp.int32, (PART, HEAD), 0).astype(jnp.float32).astype(jnp.bfloat16)
    for i in range(GROUP):
        span = slice(i * PART, (i + 1) * PART)
        first = jnp.clip(start_ref[i, half] - (begin + part) * PART, 0, PART)
        later = slot >= first.astype(jnp.float32).astype(jnp.bfloat16)
        value = value_ref[i]
        rows[span, :HEAD] = jnp.where(later, jnp.bfloat16(0), value)
        rows[span, HEAD:] = jnp.where(later, value, jnp.bfloat16(0))
        query = (code_ref[i : i + 1, :] >> 9) & (half * TOK - 1)
        weight = weight_ref[i : i + 1, :]
        for h in range(half):
            ids = lax.broadcasted_iota(jnp.int32, (TOK, PART), 0) + h * TOK
            spread[h * TOK : (h + 1) * TOK, span] = jnp.where(ids == query, weight, 0.0).astype(jnp.bfloat16)
    out_ref[...] += jnp.dot(spread[...], rows[...], preferred_element_type=jnp.float32)


def mix(codes, weights, values, begin):
    parts = values.shape[1] // PART
    return pl.pallas_call(
        functools.partial(mix_kernel, begin=begin),
        grid=(DEVS // GROUP, parts),
        in_specs=[
            pl.BlockSpec((GROUP, PART), lambda g, p: (g, begin + p)),
            pl.BlockSpec((GROUP, 128), lambda g, p: (g, CAP // 128), memory_space=pltpu.SMEM),
            pl.BlockSpec((GROUP, PART), lambda g, p: (g, begin + p)),
            pl.BlockSpec((GROUP, PART, HEAD), lambda g, p: (g, p, 0)),
        ],
        out_specs=pl.BlockSpec((HEADS // 2 * TOK, 2 * HEAD), lambda g, p: (0, 0)),
        out_shape=jax.ShapeDtypeStruct((HEADS // 2 * TOK, 2 * HEAD), jnp.float32),
        scratch_shapes=[
            pltpu.VMEM((HEADS // 2 * TOK, GROUP * PART), jnp.bfloat16),
            pltpu.VMEM((GROUP * PART, 2 * HEAD), jnp.bfloat16),
        ],
        compiler_params=pltpu.CompilerParams(vmem_limit_bytes=32 * 1024 * 1024),
        cost_estimate=cost(12 * parts),
        name="mix",
    )(codes, codes, weights, values)


def shards(queries, keys, values, mem_keys, mem_values, knn_index, block_slot, gate_bias, w_out):
    send = functools.partial(
        lax.all_to_all, axis_name=("seq", "mem"), split_axis=0, concat_axis=0, tiled=True
    )
    planes = lax.axis_size("seq")
    near = lax.axis_size("mem")
    near_queries = lax.all_gather(turn(queries[0]), "mem", axis=0, tiled=True).reshape(near, HEADS * TOK, HEAD)
    up = [(i, (i + 1) % planes) for i in range(planes)]
    down = [(i, (i - 1) % planes) for i in range(planes)]
    middle = mem_keys.shape[0] // 2
    below = lax.ppermute(mem_keys, "seq", up)
    above = lax.ppermute(mem_keys, "seq", down)
    own = jnp.concatenate([keys[0], values[0]], axis=1)
    seen = lax.all_gather(own, "seq", axis=0, tiled=True)

    lookups = knn_index[0].transpose(1, 0, 2).reshape(TOK * HEADS * TOPK // ROWS, ROWS)
    asked, places = route(lookups, block_slot)
    below, above = after(asked, below, above)
    far = jnp.concatenate(
        [lax.ppermute(below[:middle], "seq", up), lax.ppermute(above[middle:], "seq", down)], axis=0
    )
    place = lax.axis_index("seq")
    line_keys = jnp.zeros((planes * MEM_DEV, HEADS * HEAD), mem_keys.dtype)
    for back, rows in enumerate((mem_keys, below, far, above)):
        line_keys = lax.dynamic_update_slice_in_dim(line_keys, rows, (place - back) % planes * MEM_DEV, axis=0)
    wanted = lax.all_to_all(
        asked.reshape(planes, near, CAP + 128), "mem", split_axis=1, concat_axis=1, tiled=True
    )
    codes = lax.all_to_all(wanted, "seq", split_axis=0, concat_axis=0, tiled=True).reshape(DEVS, CAP + 128)
    wanted = wanted.reshape(DEVS, CAP + 128)

    query = queries[0].reshape(TOK, HEADS, HEAD)
    key_rows = seen[:, : HEADS * HEAD].reshape(-1, HEADS, HEAD)
    value_rows = seen[:, HEADS * HEAD :].reshape(-1, HEADS, HEAD)
    local = jnp.einsum("qhd,khd->hqk", query, key_rows, preferred_element_type=jnp.float32) * HEAD ** (-0.5)
    query_pos = lax.axis_index("seq") * TOK + jnp.arange(TOK, dtype=jnp.int32)
    key_pos = jnp.arange(seen.shape[0], dtype=jnp.int32)
    local = jnp.where(key_pos[None, None, :] <= query_pos[None, :, None], local, -jnp.inf)
    probs = jax.nn.softmax(local, axis=-1).astype(jnp.bfloat16)
    local_out = jnp.einsum("hqk,khd->hqd", probs, value_rows, preferred_element_type=jnp.float32)
    picked, later = pick(codes, mem_values, line_keys)
    first = send(picked)
    scored, later = score(wanted, near_queries, line_keys, later)
    scored = join(scored, first, local_out).reshape(planes, near, CAP)
    scores = lax.all_to_all(scored, "mem", split_axis=1, concat_axis=1, tiled=True).reshape(DEVS, CAP)
    last = send(later)
    weights = weigh(places, scores)
    sums = mix(asked, weights, first, 0) + mix(asked, weights, last, PARTS - 1)
    mem_out = jnp.concatenate([sums[:, :HEAD], sums[:, HEAD:]], axis=0).reshape(HEADS, TOK, HEAD)

    gate = jax.nn.sigmoid(gate_bias)[:, None, None]
    combined = (gate * mem_out + (1.0 - gate) * local_out).astype(jnp.bfloat16)
    combined = combined.transpose(1, 0, 2).reshape(TOK, HEADS * HEAD)
    mixed = jnp.dot(combined, w_out, preferred_element_type=jnp.float32).astype(jnp.bfloat16)
    return mixed[None]


def solution(mesh):
    return jax.shard_map(
        shards,
        mesh=mesh,
        in_specs=(
            P("mem", "seq", None),
            P("mem", "seq", None),
            P("mem", "seq", None),
            P(("seq", "mem"), None),
            P(("seq", "mem"), None),
            P("mem", "seq", None, None),
            P(),
            P(),
            P(),
        ),
        out_specs=P("mem", "seq", None),
        check_vma=False,
    )
```
